512 devices in a mesh: section: 4 (over x), ctx: 128 (over y, z, core).
Axes of the slice: x: 4, y: 8, z: 8, core: 2. Of those that a mesh axis runs over, the one named last changes fastest.
Arguments:
- query_in: bfloat16 [4, 2, 16384, 2048], P('section', None, 'ctx'), may hold values from -24 to 24
- key_in: bfloat16 [4, 2, 16384, 256], P('section', None, 'ctx'), may hold values from -24 to 24
- value_in: bfloat16 [4, 2, 16384, 256], P('section', None, 'ctx'), may hold values from -5 to 5
- doc_ids: int32 [2, 16384], replicated, may hold values from 0 to 159, never falling along the last dimension, each value on 1 to 128 neighbouring positions
- out_grad: bfloat16 [2, 16384, 2048], P(None, 'ctx'), may hold values from -5 to 5
Outputs:
- attention: bfloat16 [4, 2, 16384, 2048], P('section', None, 'ctx')
- query_grad: bfloat16 [4, 2, 16384, 2048], P('section', None, 'ctx')
- key_grad: bfloat16 [4, 2, 16384, 256], P('section', None, 'ctx')
- value_grad: bfloat16 [4, 2, 16384, 256], P('section', None, 'ctx')
The draws below stay inside these ranges and needn't reach their ends.
Inputs may be any that keep to these rules, and one draw needn't show every extreme that they name: `doc_ids`: never falling along the tokens; each document holds 1 to 128 tokens, one exactly 128.
All inputs are finite; a program needn't handle non-finite values.
Results may differ from the reference program's by a relative error of at most 0.012.
The reference program's roundings to bfloat16 on the way count: a program that leaves them out, or rounds other values in their place, can miss the bound.
Values may be sent and summed in bfloat16 or wider, within the bound.
A program may use at most 128 MiB of HBM per device.

```python
import math
import jax
import jax.numpy as jnp
import numpy as np
from jax import lax

HD = 128
GROUP = 8
KVH = 2
TOK_DEV = 128
REACH = 1
MB = 2
SECTIONS = 4
TOKENS = 16384
MAXDOC = 128
DOCS = 160
N_CTX = 128


def draw_query_in(key, part):
    key = jax.random.fold_in(key, 3)
    full_shape = (SECTIONS, MB, TOKENS, KVH * GROUP * HD)
    return jnp.clip(jax.random.normal(key, full_shape, jnp.float32), -5.0, 5.0).astype(jnp.bfloat16)


def draw_key_in(key, part):
    key = jax.random.fold_in(key, 4)
    full_shape = (SECTIONS, MB, TOKENS, KVH * HD)
    return jnp.clip(jax.random.normal(key, full_shape, jnp.float32), -5.0, 5.0).astype(jnp.bfloat16)


def block_levels(key, shape, split, least, high):
    loudness, own = 1.0, jax.random.fold_in(key, 6)
    for position, blocks in split:
        heights = jnp.exp(jax.random.uniform(jax.random.fold_in(own, position), (blocks,), jnp.float32, least / len(split), high / len(split)))
        loudness = loudness * jnp.repeat(heights, shape[position] // blocks).reshape([-1 if axis == position else 1 for axis in range(len(shape))])
    return loudness


def length_profile(amount, total, limit, skew):
    loads = [(1 << 20) // math.isqrt(rank ** skew) + 1 for rank in range(2, amount + 1)]
    rest, counts = total - limit - (amount - 1), [1] * (amount - 1)
    while rest > 0:
        movable = [i for i in range(amount - 1) if counts[i] < limit]
        mass, remaining = sum([loads[i] for i in movable]), rest
        for i in movable:
            more = min(limit - counts[i], max(1, remaining * loads[i] // mass), rest)
            counts[i] = counts[i] + more
            rest = rest - more
    return np.array([limit] + counts)


def uneven(own_key, amount, total, limit, lean):
    if amount == 2:
        one = jax.random.randint(own_key, (), max(1, total - limit), min(limit, total - 1) + 1)
        return jnp.stack([one, total - one])
    tallies = jnp.asarray(length_profile(amount, total, limit, lean), jnp.int32)
    couples = (amount - 1) // 2
    donor, taker = tallies[1:1 + 2 * couples:2], tallies[2:2 + 2 * couples:2]
    room = jnp.minimum(donor - 1, limit - taker)
    passed = jax.random.randint(jax.random.fold_in(own_key, 1), (couples,), 0, 1 << 20) % (room + 1)
    tallies = tallies.at[1:1 + 2 * couples:2].set(donor - passed).at[2:2 + 2 * couples:2].set(taker + passed)
    return tallies[jax.random.permutation(jax.random.fold_in(own_key, 2), amount)]


def normal_values(stream_key, dims, width, reach, shards=(), held_as=jnp.bfloat16):
    values = width * jax.random.normal(stream_key, dims, jnp.float32)
    if shards:
        values = values * block_levels(stream_key, dims, shards, -0.22, 0.18)
    return jnp.clip(values, -reach, reach).astype(held_as)


def setup_inputs(seed: int = 0) -> dict:
    arg_keys = jax.random.split(jax.random.key(seed), 6)
    return {
        "query_in": draw_query_in(jax.random.fold_in(arg_keys[5], 71), 0),
        "key_in": draw_key_in(jax.random.fold_in(arg_keys[5], 71), 0),
        "value_in": normal_values(arg_keys[2], (SECTIONS, MB, TOKENS, KVH * HD), 1.0, 5.0, ((0, 4), (2, 128))),
        "doc_ids": jax.vmap(lambda own: jnp.searchsorted(jnp.cumsum(uneven(own, DOCS, TOKENS, MAXDOC, 0)), jnp.arange(TOKENS), side="right"))(jax.random.split(arg_keys[3], MB)).reshape((MB, TOKENS)).astype(jnp.int32),
        "out_grad": normal_values(arg_keys[4], (MB, TOKENS, KVH * GROUP * HD), 1.0, 5.0, ((1, 128),)),
    }


def with_front(array_in, fill_value):
    front = jnp.full((REACH * TOK_DEV,) + array_in.shape[1:], fill_value, array_in.dtype)
    return jnp.concatenate([front, array_in], axis=0)

def softmax_weights(query_rows, key_win, own_ids, win_ids):
    tok_rows = query_rows.shape[0]
    per_head = query_rows.reshape(tok_rows, KVH, GROUP, HD).astype(jnp.float32)
    key_heads = key_win.reshape(key_win.shape[0], KVH, HD).astype(jnp.float32)
    scores = jnp.einsum('tngd,knd->ngtk', per_head, key_heads) / math.sqrt(HD)
    causal = jnp.arange(key_win.shape[0])[None, :] <= jnp.arange(tok_rows)[:, None] + REACH * tok_rows
    allowed = (win_ids[None, :] == own_ids[:, None]) & causal
    scores = jnp.where(allowed[None, None], scores, -1e+30)
    row_max = lax.optimization_barrier(jnp.max(scores, axis=3, keepdims=True))
    lifted = jnp.exp(scores - row_max)
    return lifted / lax.optimization_barrier(jnp.sum(lifted, axis=3, keepdims=True))

def block_slices(mixed_rows, key_pad, value_pad, id_pad, doc_row, block_no):
    offset = (block_no * TOK_DEV).astype(jnp.int32)
    win_len = (REACH + 1) * TOK_DEV
    query_rows = lax.dynamic_slice_in_dim(mixed_rows, offset, TOK_DEV, 0)
    own_ids = lax.dynamic_slice_in_dim(doc_row, offset, TOK_DEV, 0)
    key_win = lax.dynamic_slice_in_dim(key_pad, offset, win_len, 0)
    value_win = lax.dynamic_slice_in_dim(value_pad, offset, win_len, 0)
    win_ids = lax.dynamic_slice_in_dim(id_pad, offset, win_len, 0)
    return (offset, query_rows, own_ids, key_win, value_win, win_ids)

def layer_forward(mixed_rows, key_rows, value_rows, doc_row):
    key_pad = with_front(key_rows, 0)
    value_pad = with_front(value_rows, 0)
    id_pad = with_front(doc_row, -1)

    def one_block(block_no):
        offset, query_rows, own_ids, key_win, value_win, win_ids = block_slices(mixed_rows, key_pad, value_pad, id_pad, doc_row, block_no)
        weights = softmax_weights(query_rows, key_win, own_ids, win_ids)
        rounded = lax.optimization_barrier(weights.astype(jnp.bfloat16)).astype(jnp.float32)
        value_heads = value_win.reshape(value_win.shape[0], KVH, HD).astype(jnp.float32)
        result = jnp.einsum('ngtk,knd->tngd', rounded, value_heads)
        return result.reshape(TOK_DEV, KVH * GROUP * HD).astype(jnp.bfloat16)
    blocks_out = lax.map(one_block, jnp.arange(N_CTX, dtype=jnp.int32))
    return blocks_out.reshape(TOKENS, KVH * GROUP * HD)

def layer_backward(mixed_rows, key_rows, value_rows, doc_row, grad_rows):
    key_pad = with_front(key_rows, 0)
    value_pad = with_front(value_rows, 0)
    id_pad = with_front(doc_row, -1)
    win_len = (REACH + 1) * TOK_DEV

    def one_block(totals, block_no):
        key_acc, value_acc = totals
        offset, query_rows, own_ids, key_win, value_win, win_ids = block_slices(mixed_rows, key_pad, value_pad, id_pad, doc_row, block_no)
        weights = softmax_weights(query_rows, key_win, own_ids, win_ids)
        rounded = lax.optimization_barrier(weights.astype(jnp.bfloat16)).astype(jnp.float32)
        grad_head = lax.dynamic_slice_in_dim(grad_rows, offset, TOK_DEV, 0).reshape(TOK_DEV, KVH, GROUP, HD).astype(jnp.float32)
        query_head = query_rows.reshape(TOK_DEV, KVH, GROUP, HD).astype(jnp.float32)
        key_heads = key_win.reshape(win_len, KVH, HD).astype(jnp.float32)
        value_heads = value_win.reshape(win_len, KVH, HD).astype(jnp.float32)
        weight_grad = jnp.einsum('tngd,knd->ngtk', grad_head, value_heads)
        row_dot = lax.optimization_barrier(jnp.sum(weights * weight_grad, axis=3, keepdims=True))
        score_grad = weights * (weight_grad - row_dot) / math.sqrt(HD)
        score_grad = lax.optimization_barrier(score_grad.astype(jnp.bfloat16)).astype(jnp.float32)
        input_grad = jnp.einsum('ngtk,knd->tngd', score_grad, key_heads)
        input_grad = input_grad.reshape(TOK_DEV, KVH * GROUP * HD).astype(jnp.bfloat16)
        key_part = jnp.einsum('ngtk,tngd->knd', score_grad, query_head).reshape(win_len, KVH * HD)
        value_part = jnp.einsum('ngtk,tngd->knd', rounded, grad_head).reshape(win_len, KVH * HD)
        key_acc = lax.dynamic_update_slice_in_dim(key_acc, lax.dynamic_slice_in_dim(key_acc, offset, win_len, 0) + key_part, offset, 0)
        value_acc = lax.dynamic_update_slice_in_dim(value_acc, lax.dynamic_slice_in_dim(value_acc, offset, win_len, 0) + value_part, offset, 0)
        return ((key_acc, value_acc), input_grad)
    zero_acc = jnp.zeros((TOKENS + REACH * TOK_DEV, KVH * HD), jnp.float32)
    (key_acc, value_acc), grads_out = lax.scan(one_block, (zero_acc, zero_acc), jnp.arange(N_CTX, dtype=jnp.int32))
    key_out = key_acc[REACH * TOK_DEV:].astype(jnp.bfloat16)
    value_out = value_acc[REACH * TOK_DEV:].astype(jnp.bfloat16)
    return (grads_out.reshape(TOKENS, KVH * GROUP * HD), key_out, value_out)

def stacked(by_pair):
    return jnp.stack([jnp.stack([by_pair[section_no, micro_no] for micro_no in range(MB)]) for section_no in range(SECTIONS)])

def reference(query_in, key_in, value_in, doc_ids, out_grad):
    mixed_by, attention_by = ({}, {})
    for micro_no in range(MB):
        carried = jnp.zeros((TOKENS, KVH * GROUP * HD), jnp.float32)
        for section_no in range(SECTIONS):
            mixed_rows = (query_in[section_no, micro_no].astype(jnp.float32) + carried).astype(jnp.bfloat16)
            result = layer_forward(mixed_rows, key_in[section_no, micro_no], value_in[section_no, micro_no], doc_ids[micro_no])
            mixed_by[section_no, micro_no] = mixed_rows
            attention_by[section_no, micro_no] = result
            carried = result.astype(jnp.float32)
    query_by, key_by, value_by = ({}, {}, {})
    for micro_no in range(MB):
        grad_rows = out_grad[micro_no]
        for section_no in reversed(range(SECTIONS)):
            input_grad, key_part, value_part = layer_backward(mixed_by[section_no, micro_no], key_in[section_no, micro_no], value_in[section_no, micro_no], doc_ids[micro_no], grad_rows)
            query_by[section_no, micro_no] = input_grad
            key_by[section_no, micro_no] = key_part
            value_by[section_no, micro_no] = value_part
            grad_rows = input_grad
    return (stacked(attention_by), stacked(query_by), stacked(key_by), stacked(value_by))
```

```python
import functools
import math

import jax
import jax.numpy as jnp
from jax import lax
from jax.experimental import pallas as pl
from jax.experimental.pallas import tpu as pltpu
from jax.sharding import PartitionSpec as P

HD = 128
GROUP = 8
KVH = 2
HEADS = GROUP * KVH
MB = 2
TOK = 128
G = 1
CPG = GROUP // G
NGRP = MB * KVH
NCH = NGRP * CPG
ROWS = G * TOK
DELAY = 3
MESH = pl.DeviceIdType.MESH
SCALE = 1.0 / math.sqrt(HD)
EXP2_SCALE = math.log2(math.e) / math.sqrt(HD)
NT = (((1,), (1,)), ((), ()))
NN = (((1,), (0,)), ((), ()))
TN = (((0,), (0,)), ((), ()))


def dot(a, b, dims):
    return lax.dot_general(a, b, dims, preferred_element_type=jnp.float32)


def kernel(
    sections,
    shards_n,
    q_hbm,
    k_hbm,
    v_hbm,
    ids_hbm,
    og_hbm,
    att_hbm,
    qg_hbm,
    kg_hbm,
    vg_hbm,
    qbuf,
    frecv,
    mixbuf,
    wbuf,
    pbuf,
    obuf,
    brecv,
    dqbuf,
    kcat,
    vcat,
    bias,
    own_ids,
    prev_ids,
    dkt,
    dvt,
    part_send,
    part_recv,
    kgbuf,
    vgbuf,
    q_sem,
    kv_sem,
    ids_sem,
    halo_send,
    halo_recv,
    f_send,
    f_recv,
    b_send,
    b_recv,
    part_send_sem,
    part_recv_sem,
    out_sem,
    kvout_sem,
):
    s = lax.axis_index("section")
    c = lax.axis_index("ctx")
    last = sections - 1
    first_shard = c == 0
    last_shard = c == shards_n - 1

    barrier = pltpu.get_barrier_semaphore()
    for peer in (
        (lax.rem(s + 1, sections), c),
        (lax.rem(s + sections - 1, sections), c),
        (s, lax.rem(c + 1, shards_n)),
        (s, lax.rem(c + shards_n - 1, shards_n)),
    ):
        pl.semaphore_signal(barrier, inc=1, device_id=peer, device_id_type=MESH)

    own_at = pl.multiple_of(c * TOK, TOK)
    prev_at = pl.multiple_of(jnp.maximum(c - 1, 0) * TOK, TOK)
    own_copy = pltpu.make_async_copy(ids_hbm.at[:, pl.ds(own_at, TOK)], own_ids, ids_sem.at[0])
    prev_copy = pltpu.make_async_copy(ids_hbm.at[:, pl.ds(prev_at, TOK)], prev_ids, ids_sem.at[1])
    own_copy.start()
    prev_copy.start()

    def head_cols(ref, chunk, head):
        m = chunk // (KVH * CPG)
        col = lax.rem(chunk, KVH * CPG) * G + head
        return ref.at[m, :, pl.ds(pl.multiple_of(col * HD, HD), HD)]

    def head_rows(ref, chunk, head):
        return ref.at[chunk, pl.ds(head * TOK, TOK)]

    for grp in range(NGRP):
        m, n = divmod(grp, KVH)
        for which, (src, dst) in enumerate(((k_hbm, kcat), (v_hbm, vcat))):
            pltpu.make_async_copy(
                src.at[m, :, pl.ds(n * HD, HD)], dst.at[grp, pl.ds(TOK, TOK)], kv_sem.at[which]
            ).start()

    @pl.loop(0, NCH)
    def _(i):
        for head in range(G):
            pltpu.make_async_copy(head_cols(q_hbm, i, head), head_rows(qbuf, i, head), q_sem).start()

    @pl.when(s == last)
    def _():
        @pl.loop(0, NCH)
        def _(i):
            for head in range(G):
                pltpu.make_async_copy(
                    head_cols(og_hbm, i, head), head_rows(brecv, i, head), b_recv.at[i]
                ).start()

    dkt[...] = jnp.zeros_like(dkt)
    dvt[...] = jnp.zeros_like(dvt)

    @pl.when(s == 0)
    def _():
        frecv[...] = jnp.zeros_like(frecv)

    @pl.when(first_shard)
    def _():
        for grp in range(NGRP):
            kcat[grp, :TOK] = jnp.zeros((TOK, HD), jnp.bfloat16)
            vcat[grp, :TOK] = jnp.zeros((TOK, HD), jnp.bfloat16)

    pl.semaphore_wait(barrier, 4)

    def halo(grp, which):
        m, n = divmod(grp, KVH)
        src, dst = ((k_hbm, kcat), (v_hbm, vcat))[which]
        return pltpu.make_async_remote_copy(
            src_ref=src.at[m, :, pl.ds(n * HD, HD)],
            dst_ref=dst.at[grp, pl.ds(0, TOK)],
            send_sem=halo_send.at[2 * grp + which],
            recv_sem=halo_recv.at[2 * grp + which],
            device_id=(s, jnp.minimum(c + 1, shards_n - 1)),
            device_id_type=MESH,
        )

    @pl.when(jnp.logical_not(last_shard))
    def _():
        for grp in range(NGRP):
            for which in range(2):
                halo(grp, which).start()

    row = lax.broadcasted_iota(jnp.int32, (TOK, TOK), 0)
    col = lax.broadcasted_iota(jnp.int32, (TOK, TOK), 1)
    own_copy.wait()
    prev_copy.wait()
    for m in range(MB):
        own_row = jnp.broadcast_to(own_ids[m : m + 1, :], (TOK, TOK)).astype(jnp.float32)
        prev_row = jnp.broadcast_to(prev_ids[m : m + 1, :], (TOK, TOK)).astype(jnp.float32)
        prev_row = jnp.where(first_shard, -1.0, prev_row)
        seen = jnp.where(col <= row, own_row, prev_row)
        bias[m] = jnp.where(seen == own_row.T, 0.0, -1e30)
    pltpu.make_async_copy(qbuf, qbuf, q_sem).wait()
    for which, dst in enumerate((kcat, vcat)):
        view = dst.at[:, pl.ds(TOK, TOK)]
        pltpu.make_async_copy(view, view, kv_sem.at[which]).wait()

    def tri():
        rows = lax.broadcasted_iota(jnp.int32, (ROWS, TOK), 0)
        cols = lax.broadcasted_iota(jnp.int32, (ROWS, TOK), 1)
        return cols <= lax.rem(rows, TOK)

    def split(weights):
        own = tri()
        prev_half = jnp.where(own, 0.0, weights).astype(jnp.bfloat16)
        own_half = jnp.where(own, weights, 0.0).astype(jnp.bfloat16)
        return jnp.concatenate([prev_half, own_half], axis=1)

    def merge(wide):
        return jnp.where(tri(), wide[:, TOK:], wide[:, :TOK])

    def f_copy(i):
        return pltpu.make_async_remote_copy(
            src_ref=obuf.at[i],
            dst_ref=frecv.at[i],
            send_sem=f_send,
            recv_sem=f_recv.at[i],
            device_id=(jnp.minimum(s + 1, last), c),
            device_id_type=MESH,
        )

    def b_copy(i):
        return pltpu.make_async_remote_copy(
            src_ref=dqbuf.at[i],
            dst_ref=brecv.at[i],
            send_sem=b_send,
            recv_sem=b_recv.at[i],
            device_id=(jnp.maximum(s - 1, 0), c),
            device_id_type=MESH,
        )

    def part_copy(grp):
        return pltpu.make_async_remote_copy(
            src_ref=part_send.at[grp],
            dst_ref=part_recv.at[grp],
            send_sem=part_send_sem,
            recv_sem=part_recv_sem.at[grp],
            device_id=(s, jnp.maximum(c - 1, 0)),
            device_id_type=MESH,
        )

    def wait_forward(i):
        grp = i // CPG

        @pl.when(jnp.logical_and(lax.rem(i, CPG) == 0, jnp.logical_not(first_shard)))
        def _():
            for which, dst in enumerate((kcat, vcat)):
                view = dst.at[grp, pl.ds(0, TOK)]
                pltpu.make_async_copy(view, view, halo_recv.at[2 * grp + which]).wait()

        @pl.when(s > 0)
        def _():
            pltpu.make_async_copy(frecv.at[i], frecv.at[i], f_recv.at[i]).wait()

    def wait_backward(i):
        pltpu.make_async_copy(brecv.at[i], brecv.at[i], b_recv.at[i]).wait()

    def forward(i):
        grp = i // CPG
        mixed = (qbuf[i].astype(jnp.float32) + frecv[i].astype(jnp.float32)).astype(jnp.bfloat16)
        scores = merge(dot(mixed, kcat[grp], NT))
        mask = bias[grp // KVH]
        scores = scores + (mask if G == 1 else jnp.concatenate([mask] * G, axis=0))
        lifted = jnp.exp2((scores - jnp.max(scores, axis=1, keepdims=True)) * EXP2_SCALE)
        weights = lifted * (1.0 / jnp.sum(lifted, axis=1, keepdims=True))
        wide = split(weights)
        out = dot(wide, vcat[grp], NN).astype(jnp.bfloat16)
        return mixed, weights, wide, out

    def store_forward(i, results):
        mixbuf[i], wbuf[i], pbuf[i], obuf[i] = results

    def send_forward(i):
        @pl.when(s < last)
        def _():
            f_copy(i).start()

        for head in range(G):
            pltpu.make_async_copy(head_rows(obuf, i, head), head_cols(att_hbm, i, head), out_sem.at[0]).start()

    def backward(i):
        grp = i // CPG
        grad = brecv[i]
        weights = wbuf[i]
        weight_grad = merge(dot(grad, vcat[grp], NT))
        row_dot = jnp.sum(weights * weight_grad, axis=1, keepdims=True)
        wide = split(weights * (weight_grad - row_dot) * SCALE)
        return wide, dot(wide, kcat[grp], NN).astype(jnp.bfloat16)

    def kv_terms(i, wide, mixed, probs):
        return dot(mixed, wide, TN), dot(brecv[i], probs, TN)

    def send_backward(i):
        @pl.when(s > 0)
        def _():
            b_copy(i).start()

        for head in range(G):
            pltpu.make_async_copy(head_rows(dqbuf, i, head), head_cols(qg_hbm, i, head), out_sem.at[1]).start()

    def finish_group(i):
        grp = i // CPG

        @pl.when(lax.rem(i, CPG) == CPG - 1)
        def _():
            @pl.when(jnp.logical_not(first_shard))
            def _():
                part_send[grp, 0] = dkt[grp, :, :TOK].astype(jnp.bfloat16)
                part_send[grp, 1] = dvt[grp, :, :TOK].astype(jnp.bfloat16)
                part_copy(grp).start()

    warm = 2 * DELAY * (last - s) + 1

    @pl.loop(0, warm)
    def _(t):
        wait_forward(t)
        store_forward(t, forward(t))
        send_forward(t)

    @pl.loop(warm, NCH)
    def _(t):
        b = t - warm
        wait_forward(t)
        wait_backward(b)
        grp = b // CPG
        mixed, probs = mixbuf[b], pbuf[b]
        wide, grad_out = backward(b)
        dqbuf[b] = grad_out
        dk, dv = kv_terms(b, wide, mixed, probs)
        dkt[grp] += dk
        dvt[grp] += dv
        store_forward(t, forward(t))
        send_forward(t)
        send_backward(b)
        finish_group(b)

    @pl.loop(NCH, NCH + warm)
    def _(t):
        b = t - warm
        wait_backward(b)
        grp = b // CPG
        wide, grad_out = backward(b)
        dqbuf[b] = grad_out
        send_backward(b)
        dk, dv = kv_terms(b, wide, mixbuf[b], pbuf[b])
        dkt[grp] += dk
        dvt[grp] += dv
        finish_group(b)

    for grp in range(NGRP):
        m, n = divmod(grp, KVH)

        @pl.when(jnp.logical_not(last_shard))
        def _():
            pltpu.make_async_copy(part_recv.at[grp], part_recv.at[grp], part_recv_sem.at[grp]).wait()

        for which, (acc, dst) in enumerate(((dkt, kgbuf), (dvt, vgbuf))):
            extra = jnp.where(last_shard, 0.0, part_recv[grp, which].astype(jnp.float32))
            dst[m, :, n * HD : (n + 1) * HD] = (acc[grp, :, TOK:] + extra).T.astype(jnp.bfloat16)
    kv_out = (
        pltpu.make_async_copy(kgbuf, kg_hbm, kvout_sem.at[0]),
        pltpu.make_async_copy(vgbuf, vg_hbm, kvout_sem.at[1]),
    )
    for copy in kv_out:
        copy.start()

    @pl.when(jnp.logical_not(last_shard))
    def _():
        for grp in range(NGRP):
            for which in range(2):
                halo(grp, which).wait_send()

    @pl.when(jnp.logical_not(first_shard))
    def _():
        pltpu.make_async_copy(part_send, part_send, part_send_sem).wait()

    @pl.when(s < last)
    def _():
        pltpu.make_async_copy(obuf, obuf, f_send).wait()

    @pl.when(s > 0)
    def _():
        pltpu.make_async_copy(dqbuf, dqbuf, b_send).wait()

    pltpu.make_async_copy(obuf, obuf, out_sem.at[0]).wait()
    pltpu.make_async_copy(dqbuf, dqbuf, out_sem.at[1]).wait()
    for copy in kv_out:
        copy.wait()


def shards(query_in, key_in, value_in, doc_ids, out_grad):
    sections = lax.axis_size("section")
    shards_n = lax.axis_size("ctx")
    bf16, f32 = jnp.bfloat16, jnp.float32
    feat, kv = HEADS * HD, KVH * HD
    hbm = pl.BlockSpec(memory_space=pl.ANY)
    dma = pltpu.SemaphoreType.DMA
    att, qg, kg, vg = pl.pallas_call(
        functools.partial(kernel, sections, shards_n),
        out_shape=(
            jax.ShapeDtypeStruct((MB, TOK, feat), bf16),
            jax.ShapeDtypeStruct((MB, TOK, feat), bf16),
            jax.ShapeDtypeStruct((MB, TOK, kv), bf16),
            jax.ShapeDtypeStruct((MB, TOK, kv), bf16),
        ),
        in_specs=[hbm] * 5,
        out_specs=[hbm] * 4,
        scratch_shapes=[
            pltpu.VMEM((NCH, ROWS, HD), bf16),
            pltpu.VMEM((NCH, ROWS, HD), bf16),
            pltpu.VMEM((NCH, ROWS, HD), bf16),
            pltpu.VMEM((NCH, ROWS, TOK), f32),
            pltpu.VMEM((NCH, ROWS, 2 * TOK), bf16),
            pltpu.VMEM((NCH, ROWS, HD), bf16),
            pltpu.VMEM((NCH, ROWS, HD), bf16),
            pltpu.VMEM((NCH, ROWS, HD), bf16),
            pltpu.VMEM((NGRP, 2 * TOK, HD), bf16),
            pltpu.VMEM((NGRP, 2 * TOK, HD), bf16),
            pltpu.VMEM((MB, TOK, TOK), f32),
            pltpu.VMEM((MB, TOK), jnp.int32),
            pltpu.VMEM((MB, TOK), jnp.int32),
            pltpu.VMEM((NGRP, HD, 2 * TOK), f32),
            pltpu.VMEM((NGRP, HD, 2 * TOK), f32),
            pltpu.VMEM((NGRP, 2, HD, TOK), bf16),
            pltpu.VMEM((NGRP, 2, HD, TOK), bf16),
            pltpu.VMEM((MB, TOK, kv), bf16),
            pltpu.VMEM((MB, TOK, kv), bf16),
            dma,
            dma((2,)),
            dma((2,)),
            dma((2 * NGRP,)),
            dma((2 * NGRP,)),
            dma,
            dma((NCH,)),
            dma,
            dma((NCH,)),
            dma,
            dma((NGRP,)),
            dma((2,)),
            dma((2,)),
        ],
        compiler_params=pltpu.CompilerParams(
            collective_id=0, has_side_effects=True, vmem_limit_bytes=40 * 1024 * 1024
        ),
        cost_estimate=pl.CostEstimate(flops=2_000_000_000, bytes_accessed=5_000_000, transcendentals=600_000),
    )(query_in[0], key_in[0], value_in[0], doc_ids, out_grad)
    return (att[None], qg[None], kg[None], vg[None])


def solution(mesh):
    split = P("section", None, "ctx", None)
    return jax.shard_map(
        shards,
        mesh=mesh,
        in_specs=(split, split, split, P(), P(None, "ctx", None)),
        out_specs=(split, split, split, split),
        check_vma=False,
    )
```

```python
import functools
import math

import jax
import jax.numpy as jnp
from jax import lax
from jax.experimental import pallas as pl
from jax.experimental.pallas import tpu as pltpu
from jax.sharding import PartitionSpec as P

HD = 128
GROUP = 8
KVH = 2
HEADS = GROUP * KVH
MB = 2
TOK = 128
LAYERS = 4
NGRP = MB * KVH
G = 4
NU = GROUP // G
COLS = G * HD
ROWS = G * TOK
SLOTS = 4
MESH = pl.DeviceIdType.MESH
SCALE = 1.0 / math.sqrt(HD)
EXP2_SCALE = math.log2(math.e) / math.sqrt(HD)
NT = (((1,), (1,)), ((), ()))
NN = (((1,), (0,)), ((), ()))
TN = (((0,), (0,)), ((), ()))

PLACE = (
    (0, 0, 0, 0),
    (1, 1, 1, 1),
    (2, 2, 2, 2),
    (3, 3, 3, 3),
)
ORDER = (
    (0, 1, 4, 8, 12, 28, 24, 20, 5, 16, 9, 13, 29, 25, 21, 17),
    (0, 4, 8, 12, 28, 24, 20, 16, 1, 5, 9, 13, 29, 25, 21, 17),
    (0, 4, 8, 12, 28, 24, 20, 16, 1, 5, 9, 13, 29, 25, 21, 17),
    (0, 4, 8, 12, 28, 24, 20, 16, 1, 5, 9, 13, 29, 25, 21, 17),
)
PAIRS = tuple(
    tuple((g, l) for g in range(NGRP) for l in range(LAYERS) if PLACE[g][l] == x) for x in range(LAYERS)
)
SLOT = tuple(tuple(PAIRS[PLACE[g][l]].index((g, l)) for l in range(LAYERS)) for g in range(NGRP))
STEPS = 2 * SLOTS * NU
PER_WORD = 6


def packed(numbers):
    return tuple(
        sum(n << (5 * j) for j, n in enumerate(numbers[i : i + PER_WORD])) for i in range(0, STEPS, PER_WORD)
    )


def pair_code(g, l):
    after, before = min(l + 1, LAYERS - 1), max(l - 1, 0)
    fields = (g, l, PLACE[g][after], SLOT[g][after], PLACE[g][before], SLOT[g][before])
    return sum(n << (2 * j) for j, n in enumerate(fields))


def choose(index, values):
    out = values[-1]
    for j in range(len(values) - 2, -1, -1):
        if not (isinstance(out, int) and isinstance(values[j], int) and out == values[j]):
            out = jnp.where(index == j, values[j], out)
    return out


def field(code, j):
    return lax.rem(lax.shift_right_logical(code, jnp.int32(2 * j)), 4)


def dot(a, b, dims):
    return lax.dot_general(a, b, dims, preferred_element_type=jnp.float32)


def stack_heads(x):
    return jnp.concatenate([x[:, h * HD : (h + 1) * HD] for h in range(G)], axis=0)


def side_by_side(x):
    return jnp.concatenate([x[h * TOK : (h + 1) * TOK] for h in range(G)], axis=1)


def kernel(
    shards_n,
    q_hbm,
    k_hbm,
    v_hbm,
    ids_hbm,
    og_hbm,
    att_hbm,
    qg_hbm,
    kg_hbm,
    vg_hbm,
    qbuf,
    fin,
    gin,
    obuf,
    dqbuf,
    mixbuf,
    wbuf,
    pbuf,
    kcat,
    vcat,
    bias,
    own_ids,
    prev_ids,
    dkt,
    dvt,
    part_send,
    part_recv,
    kvout,
    ids_sem,
    q_send,
    q_recv,
    kv_send,
    kv_recv,
    halo_send,
    halo_recv,
    f_send,
    f_recv,
    b_send,
    b_recv,
    part_send_sem,
    part_recv_sem,
    home_send,
    home_recv,
):
    x = lax.axis_index("section")
    c = lax.axis_index("ctx")
    first_shard = c == 0
    last_shard = c == shards_n - 1

    barrier = pltpu.get_barrier_semaphore()
    for d in range(1, LAYERS):
        pl.semaphore_signal(barrier, inc=1, device_id=(lax.rem(x + d, LAYERS), c), device_id_type=MESH)

    @pl.when(jnp.logical_not(first_shard))
    def _():
        pl.semaphore_signal(barrier, inc=1, device_id=(x, jnp.maximum(c - 1, 0)), device_id_type=MESH)

    codes = [choose(x, [pair_code(*PAIRS[s][slot]) for s in range(LAYERS)]) for slot in range(SLOTS)]
    words = [
        choose(x, [packed(ORDER[s])[w] for s in range(LAYERS)]) for w in range((STEPS + PER_WORD - 1) // PER_WORD)
    ]

    def move(src, dst, send_sem, recv_sem, section):
        return pltpu.make_async_remote_copy(
            src_ref=src,
            dst_ref=dst,
            send_sem=send_sem,
            recv_sem=recv_sem,
            device_id=(section, c),
            device_id_type=MESH,
        )

    def wait_for(ref, sem):
        pltpu.make_async_copy(ref, ref, sem).wait()

    def columns(ref, group, unit):
        m, n = group // KVH, lax.rem(group, KVH)
        return ref.at[m, :, pl.ds(pl.multiple_of(n * GROUP * HD + unit * COLS, COLS), COLS)]

    def kv_columns(ref, group):
        m, n = group // KVH, lax.rem(group, KVH)
        return ref.at[m, :, pl.ds(pl.multiple_of(n * HD, HD), HD)]

    places = [(choose(x, PLACE[g]), choose(x, SLOT[g])) for g in range(NGRP)]

    own_at = pl.multiple_of(c * TOK, TOK)
    prev_at = pl.multiple_of(jnp.maximum(c - 1, 0) * TOK, TOK)
    own_copy = pltpu.make_async_copy(ids_hbm.at[:, pl.ds(own_at, TOK)], own_ids, ids_sem.at[0])
    prev_copy = pltpu.make_async_copy(ids_hbm.at[:, pl.ds(prev_at, TOK)], prev_ids, ids_sem.at[1])
    own_copy.start()
    prev_copy.start()

    for g, (section, slot) in enumerate(places):

        @pl.when(section == x)
        def _():
            for which, (src, dst) in enumerate(((k_hbm, kcat), (v_hbm, vcat))):
                pltpu.make_async_copy(
                    kv_columns(src, g), dst.at[slot, pl.ds(TOK, TOK)], kv_recv.at[2 * slot + which]
                ).start()
            for u in range(NU):
                pltpu.make_async_copy(columns(q_hbm, g, u), qbuf.at[slot, u], q_recv.at[slot * NU + u]).start()

    for slot in range(SLOTS):

        @pl.when(field(codes[slot], 1) == LAYERS - 1)
        def _():
            for u in range(NU):
                pltpu.make_async_copy(
                    columns(og_hbm, field(codes[slot], 0), u), gin.at[slot, u], b_recv.at[slot * NU + u]
                ).start()

    dkt[...] = jnp.zeros_like(dkt)
    dvt[...] = jnp.zeros_like(dvt)

    @pl.when(first_shard)
    def _():
        for slot in range(SLOTS):
            kcat[slot, :TOK] = jnp.zeros((TOK, HD), jnp.bfloat16)
            vcat[slot, :TOK] = jnp.zeros((TOK, HD), jnp.bfloat16)

    pl.semaphore_wait(barrier, jnp.where(last_shard, LAYERS - 1, LAYERS))

    def kv_move(g, which):
        section, slot = places[g]
        src, dst = ((k_hbm, kcat), (v_hbm, vcat))[which]
        return move(
            kv_columns(src, g),
            dst.at[slot, pl.ds(TOK, TOK)],
            kv_send.at[2 * g + which],
            kv_recv.at[2 * slot + which],
            section,
        )

    def q_move(g, u):
        section, slot = places[g]
        return move(
            columns(q_hbm, g, u), qbuf.at[slot, u], q_send.at[g * NU + u], q_recv.at[slot * NU + u], section
        )

    for g in range(NGRP):

        @pl.when(places[g][0] != x)
        def _():
            for which in range(2):
                kv_move(g, which).start()

    for u in range(NU):
        for g in range(NGRP):

            @pl.when(places[g][0] != x)
            def _():
                q_move(g, u).start()

    row = lax.broadcasted_iota(jnp.int32, (TOK, TOK), 0)
    col = lax.broadcasted_iota(jnp.int32, (TOK, TOK), 1)
    own_copy.wait()
    prev_copy.wait()
    for m in range(MB):
        own_row = jnp.broadcast_to(own_ids[m : m + 1, :], (TOK, TOK)).astype(jnp.float32)
        prev_row = jnp.broadcast_to(prev_ids[m : m + 1, :], (TOK, TOK)).astype(jnp.float32)
        prev_row = jnp.where(first_shard, -1.0, prev_row)
        seen = jnp.where(col <= row, own_row, prev_row)
        bias[m] = jnp.where(seen == own_row.T, 0.0, -1e30)

    def halo(slot, which):
        dst = (kcat, vcat)[which]
        return pltpu.make_async_remote_copy(
            src_ref=dst.at[slot, pl.ds(TOK, TOK)],
            dst_ref=dst.at[slot, pl.ds(0, TOK)],
            send_sem=halo_send.at[2 * slot + which],
            recv_sem=halo_recv.at[2 * slot + which],
            device_id=(x, jnp.minimum(c + 1, shards_n - 1)),
            device_id_type=MESH,
        )

    for slot in range(SLOTS):
        for which, dst in enumerate((kcat, vcat)):
            wait_for(dst.at[slot, pl.ds(TOK, TOK)], kv_recv.at[2 * slot + which])

        @pl.when(jnp.logical_not(last_shard))
        def _():
            for which in range(2):
                halo(slot, which).start()

    @pl.when(jnp.logical_not(first_shard))
    def _():
        for slot in range(SLOTS):
            for which, dst in enumerate((kcat, vcat)):
                wait_for(dst.at[slot, pl.ds(0, TOK)], halo_recv.at[2 * slot + which])

    def tri():
        rows = lax.broadcasted_iota(jnp.int32, (ROWS, TOK), 0)
        cols = lax.broadcasted_iota(jnp.int32, (ROWS, TOK), 1)
        return cols <= lax.rem(rows, TOK)

    def split(weights):
        own = tri()
        prev_half = jnp.where(own, 0.0, weights).astype(jnp.bfloat16)
        own_half = jnp.where(own, weights, 0.0).astype(jnp.bfloat16)
        return jnp.concatenate([prev_half, own_half], axis=1)

    def merge(wide):
        return jnp.where(tri(), wide[:, TOK:], wide[:, :TOK])

    def deliver(buf, dst, code, index, kind, remote, local):
        group, layer = field(code, 0), field(code, 1)
        slot, u = index // NU, lax.rem(index, NU)
        src, dst = buf.at[slot, u], columns(dst, group, u)

        @pl.when(layer != x)
        def _():
            remote(move(src, dst, home_send.at[kind, index], home_recv.at[kind], layer))

        if local is not None:

            @pl.when(layer == x)
            def _():
                local(pltpu.make_async_copy(src, dst, home_recv.at[kind]))

    def pass_on(buf, dst, send, recv, code, index, forward, act):
        layer = field(code, 1)
        section, slot = (field(code, 2), field(code, 3)) if forward else (field(code, 4), field(code, 5))
        more = layer < LAYERS - 1 if forward else layer > 0
        own_slot, u = index // NU, lax.rem(index, NU)

        @pl.when(jnp.logical_and(more, section != x))
        def _():
            act(
                move(
                    buf.at[own_slot, u], dst.at[slot, u], send.at[index], recv.at[slot * NU + u], section
                )
            )

    start = lambda copy: copy.start()
    wait_send = lambda copy: copy.wait_send()

    def task_code(t):
        word = choose(t // PER_WORD, words)
        return lax.rem(lax.shift_right_logical(word, 5 * lax.rem(t, PER_WORD)), 32)

    def forward_task(slot, u, code):
        index = slot * NU + u
        layer = field(code, 1)
        wait_for(qbuf.at[slot, u], q_recv.at[index])

        @pl.when(jnp.logical_and(layer > 0, field(code, 4) != x))
        def _():
            wait_for(fin.at[slot, u], f_recv.at[index])

        carried = stack_heads(fin[slot, u]).astype(jnp.float32)
        carried = jnp.where(layer == 0, 0.0, carried)
        mixed = (stack_heads(qbuf[slot, u]).astype(jnp.float32) + carried).astype(jnp.bfloat16)
        scores = merge(dot(mixed, kcat[slot], NT))
        mask = bias[field(code, 0) // KVH]
        scores = scores + jnp.concatenate([mask] * G, axis=0)
        lifted = jnp.exp2((scores - jnp.max(scores, axis=1, keepdims=True)) * EXP2_SCALE)
        weights = lifted * (1.0 / jnp.sum(lifted, axis=1, keepdims=True))
        wide = split(weights)
        out = side_by_side(dot(wide, vcat[slot], NN).astype(jnp.bfloat16))
        mixbuf[slot, u], wbuf[slot, u], pbuf[slot, u], obuf[slot, u] = mixed, weights, wide, out
        pass_on(obuf, fin, f_send, f_recv, code, index, True, start)
        deliver(obuf, att_hbm, code, index, 0, start, start)

        @pl.when(jnp.logical_and(layer < LAYERS - 1, field(code, 2) == x))
        def _():
            fin[field(code, 3), u] = out

    def backward_task(slot, u, code):
        index = slot * NU + u
        layer = field(code, 1)

        @pl.when(jnp.logical_or(layer == LAYERS - 1, field(code, 2) != x))
        def _():
            wait_for(gin.at[slot, u], b_recv.at[index])

        grad = stack_heads(gin[slot, u])
        weights = wbuf[slot, u]
        weight_grad = merge(dot(grad, vcat[slot], NT))
        row_dot = jnp.sum(weights * weight_grad, axis=1, keepdims=True)
        wide = split(weights * (weight_grad - row_dot) * SCALE)
        out = side_by_side(dot(wide, kcat[slot], NN).astype(jnp.bfloat16))
        dqbuf[slot, u] = out
        pass_on(dqbuf, gin, b_send, b_recv, code, index, False, start)
        deliver(dqbuf, qg_hbm, code, index, 1, start, start)

        @pl.when(jnp.logical_and(layer > 0, field(code, 4) == x))
        def _():
            gin[field(code, 5), u] = out

        dkt[slot] += dot(mixbuf[slot, u], wide, TN)
        dvt[slot] += dot(grad, pbuf[slot, u], TN)

        @pl.when(jnp.logical_and(u == NU - 1, jnp.logical_not(first_shard)))
        def _():
            part_send[slot, 0] = dkt[slot, :, :TOK].astype(jnp.bfloat16)
            part_send[slot, 1] = dvt[slot, :, :TOK].astype(jnp.bfloat16)
            part_copy(slot).start()

    def part_copy(slot):
        return pltpu.make_async_remote_copy(
            src_ref=part_send.at[slot],
            dst_ref=part_recv.at[slot],
            send_sem=part_send_sem.at[slot],
            recv_sem=part_recv_sem.at[slot],
            device_id=(x, jnp.maximum(c - 1, 0)),
            device_id_type=MESH,
        )

    @pl.loop(0, STEPS)
    def _(t):
        task = task_code(t)
        slot, u = lax.rem(task // 4, SLOTS), lax.rem(task, 4)
        code = choose(slot, codes)

        @pl.when(task < 16)
        def _():
            forward_task(slot, u, code)

        @pl.when(task >= 16)
        def _():
            backward_task(slot, u, code)

    def kv_deliver(slot, which, act, local):
        group, layer = field(codes[slot], 0), field(codes[slot], 1)
        src, dst = kvout.at[slot, which], kv_columns((kg_hbm, vg_hbm)[which], group)

        @pl.when(layer != x)
        def _():
            act(move(src, dst, home_send.at[2 + which, slot], home_recv.at[2 + which], layer))

        if local is not None:

            @pl.when(layer == x)
            def _():
                local(pltpu.make_async_copy(src, dst, home_recv.at[2 + which]))

    @pl.loop(0, SLOTS)
    def _(i):
        slot = choose(i, [choose(x, [last_slots(s)[j] for s in range(LAYERS)]) for j in range(SLOTS)])

        @pl.when(jnp.logical_not(last_shard))
        def _():
            wait_for(part_recv.at[slot], part_recv_sem.at[slot])

        for which, acc in enumerate((dkt, dvt)):
            extra = jnp.where(last_shard, 0.0, part_recv[slot, which].astype(jnp.float32))
            kvout[slot, which] = (acc[slot, :, TOK:] + extra).T.astype(jnp.bfloat16)
        code = choose(slot, codes)
        group, layer = field(code, 0), field(code, 1)
        for which, dst in enumerate((kg_hbm, vg_hbm)):
            src, dst = kvout.at[slot, which], kv_columns(dst, group)

            @pl.when(layer != x)
            def _():
                move(src, dst, home_send.at[2 + which, slot], home_recv.at[2 + which], layer).start()

            @pl.when(layer == x)
            def _():
                pltpu.make_async_copy(src, dst, home_recv.at[2 + which]).start()

    for g in range(NGRP):

        @pl.when(places[g][0] != x)
        def _():
            for which in range(2):
                kv_move(g, which).wait_send()
            for u in range(NU):
                q_move(g, u).wait_send()

    for slot in range(SLOTS):

        @pl.when(jnp.logical_not(last_shard))
        def _():
            for which in range(2):
                halo(slot, which).wait_send()

        @pl.when(jnp.logical_not(first_shard))
        def _():
            part_copy(slot).wait_send()

        for u in range(NU):
            index = slot * NU + u
            pass_on(obuf, fin, f_send, f_recv, codes[slot], index, True, wait_send)
            pass_on(dqbuf, gin, b_send, b_recv, codes[slot], index, False, wait_send)
            deliver(obuf, att_hbm, codes[slot], index, 0, wait_send, None)
            deliver(dqbuf, qg_hbm, codes[slot], index, 1, wait_send, None)
        for which in range(2):
            kv_deliver(slot, which, wait_send, None)
    for kind, dst in enumerate((att_hbm, qg_hbm, kg_hbm, vg_hbm)):
        wait_for(dst, home_recv.at[kind])


def last_slots(section):
    ends = {}
    for t, task in enumerate(ORDER[section]):
        if task >= 16:
            ends[task // 4 % SLOTS] = t
    return sorted(ends, key=ends.get)


def shards(query_in, key_in, value_in, doc_ids, out_grad):
    shards_n = lax.axis_size("ctx")
    bf16, f32 = jnp.bfloat16, jnp.float32
    feat, kv = HEADS * HD, KVH * HD
    hbm = pl.BlockSpec(memory_space=pl.ANY)
    dma = pltpu.SemaphoreType.DMA
    att, qg, kg, vg = pl.pallas_call(
        functools.partial(kernel, shards_n),
        out_shape=(
            jax.ShapeDtypeStruct((MB, TOK, feat), bf16),
            jax.ShapeDtypeStruct((MB, TOK, feat), bf16),
            jax.ShapeDtypeStruct((MB, TOK, kv), bf16),
            jax.ShapeDtypeStruct((MB, TOK, kv), bf16),
        ),
        in_specs=[hbm] * 5,
        out_specs=[hbm] * 4,
        scratch_shapes=[
            pltpu.VMEM((SLOTS, NU, TOK, COLS), bf16),
            pltpu.VMEM((SLOTS, NU, TOK, COLS), bf16),
            pltpu.VMEM((SLOTS, NU, TOK, COLS), bf16),
            pltpu.VMEM((SLOTS, NU, TOK, COLS), bf16),
            pltpu.VMEM((SLOTS, NU, TOK, COLS), bf16),
            pltpu.VMEM((SLOTS, NU, ROWS, HD), bf16),
            pltpu.VMEM((SLOTS, NU, ROWS, TOK), f32),
            pltpu.VMEM((SLOTS, NU, ROWS, 2 * TOK), bf16),
            pltpu.VMEM((SLOTS, 2 * TOK, HD), bf16),
            pltpu.VMEM((SLOTS, 2 * TOK, HD), bf16),
            pltpu.VMEM((MB, TOK, TOK), f32),
            pltpu.VMEM((MB, TOK), jnp.int32),
            pltpu.VMEM((MB, TOK), jnp.int32),
            pltpu.VMEM((SLOTS, HD, 2 * TOK), f32),
            pltpu.VMEM((SLOTS, HD, 2 * TOK), f32),
            pltpu.VMEM((SLOTS, 2, HD, TOK), bf16),
            pltpu.VMEM((SLOTS, 2, HD, TOK), bf16),
            pltpu.VMEM((SLOTS, 2, TOK, HD), bf16),
            dma((2,)),
            dma((NGRP * NU,)),
            dma((SLOTS * NU,)),
            dma((2 * NGRP,)),
            dma((2 * SLOTS,)),
            dma((2 * SLOTS,)),
            dma((2 * SLOTS,)),
            dma((SLOTS * NU,)),
            dma((SLOTS * NU,)),
            dma((SLOTS * NU,)),
            dma((SLOTS * NU,)),
            dma((SLOTS,)),
            dma((SLOTS,)),
            dma((4, SLOTS * NU)),
            dma((4,)),
        ],
        compiler_params=pltpu.CompilerParams(
            collective_id=0, has_side_effects=True, vmem_limit_bytes=60 * 1024 * 1024
        ),
        cost_estimate=pl.CostEstimate(flops=2_000_000_000, bytes_accessed=5_000_000, transcendentals=600_000),
    )(query_in[0], key_in[0], value_in[0], doc_ids, out_grad)
    return (att[None], qg[None], kg[None], vg[None])


def solution(mesh):
    split = P("section", None, "ctx", None)
    return jax.shard_map(
        shards,
        mesh=mesh,
        in_specs=(split, split, split, P(), P(None, "ctx", None)),
        out_specs=(split, split, split, split),
        check_vma=False,
    )
```

```python
import functools
import math

import jax
import jax.numpy as jnp
from jax import lax
from jax.experimental import pallas as pl
from jax.experimental.pallas import tpu as pltpu
from jax.sharding import PartitionSpec as P

HD = 128
GROUP = 8
KVH = 2
HEADS = GROUP * KVH
MB = 2
TOK = 128
LAYERS = 4
NGRP = MB * KVH
G = 4
NU = GROUP // G
COLS = G * HD
ROWS = G * TOK
SLOTS = 4
MESH = pl.DeviceIdType.MESH
SCALE = 1.0 / math.sqrt(HD)
EXP2_SCALE = math.log2(math.e) / math.sqrt(HD)
NT = (((1,), (1,)), ((), ()))
NN = (((1,), (0,)), ((), ()))
TN = (((0,), (0,)), ((), ()))

PLACE = (
    (0, 0, 0, 0),
    (1, 1, 1, 1),
    (2, 2, 2, 2),
    (3, 3, 3, 3),
)
ORDER = (
    (0, 1, 4, 8, 12, 28, 24, 20, 5, 16, 9, 13, 29, 25, 21, 17),
    (0, 4, 8, 12, 28, 24, 20, 16, 1, 5, 9, 13, 29, 25, 21, 17),
    (0, 4, 8, 12, 28, 24, 20, 16, 1, 5, 9, 13, 29, 25, 21, 17),
    (0, 4, 8, 12, 28, 24, 20, 16, 1, 5, 9, 13, 29, 25, 21, 17),
)
PAIRS = tuple(
    tuple((g, l) for g in range(NGRP) for l in range(LAYERS) if PLACE[g][l] == x) for x in range(LAYERS)
)
SLOT = tuple(tuple(PAIRS[PLACE[g][l]].index((g, l)) for l in range(LAYERS)) for g in range(NGRP))
STEPS = 2 * SLOTS * NU
PER_WORD = 6


def packed(numbers):
    return tuple(
        sum(n << (5 * j) for j, n in enumerate(numbers[i : i + PER_WORD])) for i in range(0, STEPS, PER_WORD)
    )


def pair_code(g, l):
    after, before = min(l + 1, LAYERS - 1), max(l - 1, 0)
    fields = (g, l, PLACE[g][after], SLOT[g][after], PLACE[g][before], SLOT[g][before])
    return sum(n << (2 * j) for j, n in enumerate(fields))


def choose(index, values):
    out = values[-1]
    for j in range(len(values) - 2, -1, -1):
        if not (isinstance(out, int) and isinstance(values[j], int) and out == values[j]):
            out = jnp.where(index == j, values[j], out)
    return out


def field(code, j):
    return lax.rem(lax.shift_right_logical(code, jnp.int32(2 * j)), 4)


def dot(a, b, dims):
    return lax.dot_general(a, b, dims, preferred_element_type=jnp.float32)


def stack_heads(x):
    return jnp.concatenate([x[:, h * HD : (h + 1) * HD] for h in range(G)], axis=0)


def side_by_side(x):
    return jnp.concatenate([x[h * TOK : (h + 1) * TOK] for h in range(G)], axis=1)


def kernel(
    shards_n,
    q_hbm,
    k_hbm,
    v_hbm,
    ids_hbm,
    og_hbm,
    att_hbm,
    qg_hbm,
    kg_hbm,
    vg_hbm,
    qbuf,
    fin,
    gin,
    obuf,
    dqbuf,
    mixbuf,
    wbuf,
    pbuf,
    kcat,
    vcat,
    bias,
    own_ids,
    prev_ids,
    dkt,
    dvt,
    part_send,
    part_recv,
    kvout,
    ids_sem,
    q_send,
    q_recv,
    kv_send,
    kv_recv,
    halo_send,
    halo_recv,
    f_send,
    f_recv,
    b_send,
    b_recv,
    part_send_sem,
    part_recv_sem,
    home_send,
    home_recv,
):
    x = lax.axis_index("section")
    c = lax.axis_index("ctx")
    first_shard = c == 0
    last_shard = c == shards_n - 1

    barrier = pltpu.get_barrier_semaphore()
    for d in range(1, LAYERS):
        pl.semaphore_signal(barrier, inc=1, device_id=(lax.rem(x + d, LAYERS), c), device_id_type=MESH)

    @pl.when(jnp.logical_not(first_shard))
    def _():
        pl.semaphore_signal(barrier, inc=1, device_id=(x, jnp.maximum(c - 1, 0)), device_id_type=MESH)

    codes = [choose(x, [pair_code(*PAIRS[s][slot]) for s in range(LAYERS)]) for slot in range(SLOTS)]
    words = [
        choose(x, [packed(ORDER[s])[w] for s in range(LAYERS)]) for w in range((STEPS + PER_WORD - 1) // PER_WORD)
    ]

    def move(src, dst, send_sem, recv_sem, section):
        return pltpu.make_async_remote_copy(
            src_ref=src,
            dst_ref=dst,
            send_sem=send_sem,
            recv_sem=recv_sem,
            device_id=(section, c),
            device_id_type=MESH,
        )

    def wait_for(ref, sem):
        pltpu.make_async_copy(ref, ref, sem).wait()

    def columns(ref, group, unit):
        m, n = group // KVH, lax.rem(group, KVH)
        return ref.at[m, :, pl.ds(pl.multiple_of(n * GROUP * HD + unit * COLS, COLS), COLS)]

    def kv_columns(ref, group):
        m, n = group // KVH, lax.rem(group, KVH)
        return ref.at[m, :, pl.ds(pl.multiple_of(n * HD, HD), HD)]

    places = [(choose(x, PLACE[g]), choose(x, SLOT[g])) for g in range(NGRP)]

    own_at = pl.multiple_of(c * TOK, TOK)
    prev_at = pl.multiple_of(jnp.maximum(c - 1, 0) * TOK, TOK)
    own_copy = pltpu.make_async_copy(ids_hbm.at[:, pl.ds(own_at, TOK)], own_ids, ids_sem.at[0])
    prev_copy = pltpu.make_async_copy(ids_hbm.at[:, pl.ds(prev_at, TOK)], prev_ids, ids_sem.at[1])
    own_copy.start()
    prev_copy.start()

    for g, (section, slot) in enumerate(places):

        @pl.when(section == x)
        def _():
            for which, (src, dst) in enumerate(((k_hbm, kcat), (v_hbm, vcat))):
                pltpu.make_async_copy(
                    kv_columns(src, g), dst.at[slot, pl.ds(TOK, TOK)], kv_recv.at[2 * slot + which]
                ).start()
            for u in range(NU):
                pltpu.make_async_copy(columns(q_hbm, g, u), qbuf.at[slot, u], q_recv.at[slot * NU + u]).start()

    for slot in range(SLOTS):

        @pl.when(field(codes[slot], 1) == LAYERS - 1)
        def _():
            for u in range(NU):
                pltpu.make_async_copy(
                    columns(og_hbm, field(codes[slot], 0), u), gin.at[slot, u], b_recv.at[slot * NU + u]
                ).start()

    dkt[...] = jnp.zeros_like(dkt)
    dvt[...] = jnp.zeros_like(dvt)

    @pl.when(first_shard)
    def _():
        for slot in range(SLOTS):
            kcat[slot, :TOK] = jnp.zeros((TOK, HD), jnp.bfloat16)
            vcat[slot, :TOK] = jnp.zeros((TOK, HD), jnp.bfloat16)

    pl.semaphore_wait(barrier, jnp.where(last_shard, LAYERS - 1, LAYERS))

    def kv_move(g, which):
        section, slot = g, x
        src, dst = ((k_hbm, kcat), (v_hbm, vcat))[which]
        return move(
            kv_columns(src, g),
            dst.at[slot, pl.ds(TOK, TOK)],
            kv_send.at[2 * g + which],
            kv_recv.at[2 * slot + which],
            section,
        )

    def q_move(g, u):
        section, slot = g, x
        return move(
            columns(q_hbm, g, u), qbuf.at[slot, u], q_send.at[g * NU + u], q_recv.at[slot * NU + u], section
        )

    order = [lax.rem(x + d, NGRP) for d in (2, 1, 3)]
    for g in order:
        for which in range(2):
            kv_move(g, which).start()
    for u in range(NU):
        for g in order:
            q_move(g, u).start()

    row = lax.broadcasted_iota(jnp.int32, (TOK, TOK), 0)
    col = lax.broadcasted_iota(jnp.int32, (TOK, TOK), 1)
    own_copy.wait()
    prev_copy.wait()
    for m in range(MB):
        own_row = jnp.broadcast_to(own_ids[m : m + 1, :], (TOK, TOK)).astype(jnp.float32)
        prev_row = jnp.broadcast_to(prev_ids[m : m + 1, :], (TOK, TOK)).astype(jnp.float32)
        prev_row = jnp.where(first_shard, -1.0, prev_row)
        seen = jnp.where(col <= row, own_row, prev_row)
        bias[m] = jnp.where(seen == own_row.T, 0.0, -1e30)

    def halo(slot, which):
        dst = (kcat, vcat)[which]
        return pltpu.make_async_remote_copy(
            src_ref=dst.at[slot, pl.ds(TOK, TOK)],
            dst_ref=dst.at[slot, pl.ds(0, TOK)],
            send_sem=halo_send.at[2 * slot + which],
            recv_sem=halo_recv.at[2 * slot + which],
            device_id=(x, jnp.minimum(c + 1, shards_n - 1)),
            device_id_type=MESH,
        )

    for slot in range(SLOTS):
        for which, dst in enumerate((kcat, vcat)):
            wait_for(dst.at[slot, pl.ds(TOK, TOK)], kv_recv.at[2 * slot + which])

        @pl.when(jnp.logical_not(last_shard))
        def _():
            for which in range(2):
                halo(slot, which).start()

    @pl.when(jnp.logical_not(first_shard))
    def _():
        for slot in range(SLOTS):
            for which, dst in enumerate((kcat, vcat)):
                wait_for(dst.at[slot, pl.ds(0, TOK)], halo_recv.at[2 * slot + which])

    def tri():
        rows = lax.broadcasted_iota(jnp.int32, (ROWS, TOK), 0)
        cols = lax.broadcasted_iota(jnp.int32, (ROWS, TOK), 1)
        return cols <= lax.rem(rows, TOK)

    def split(weights):
        own = tri()
        prev_half = jnp.where(own, 0.0, weights).astype(jnp.bfloat16)
        own_half = jnp.where(own, weights, 0.0).astype(jnp.bfloat16)
        return jnp.concatenate([prev_half, own_half], axis=1)

    def merge(wide):
        return jnp.where(tri(), wide[:, TOK:], wide[:, :TOK])

    def deliver(buf, dst, code, index, kind, remote, local):
        group, layer = field(code, 0), field(code, 1)
        slot, u = index // NU, lax.rem(index, NU)
        src, dst = buf.at[slot, u], columns(dst, group, u)

        @pl.when(layer != x)
        def _():
            remote(move(src, dst, home_send.at[kind, index], home_recv.at[kind], layer))

        if local is not None:

            @pl.when(layer == x)
            def _():
                local(pltpu.make_async_copy(src, dst, home_recv.at[kind]))

    def pass_on(buf, dst, send, recv, code, index, forward, act):
        layer = field(code, 1)
        section, slot = (field(code, 2), field(code, 3)) if forward else (field(code, 4), field(code, 5))
        more = layer < LAYERS - 1 if forward else layer > 0
        own_slot, u = index // NU, lax.rem(index, NU)

        @pl.when(jnp.logical_and(more, section != x))
        def _():
            act(
                move(
                    buf.at[own_slot, u], dst.at[slot, u], send.at[index], recv.at[slot * NU + u], section
                )
            )

    start = lambda copy: copy.start()
    wait_send = lambda copy: copy.wait_send()

    def task_code(t):
        word = choose(t // PER_WORD, words)
        return lax.rem(lax.shift_right_logical(word, 5 * lax.rem(t, PER_WORD)), 32)

    def forward_task(slot, u, code):
        index = slot * NU + u
        layer = field(code, 1)
        wait_for(qbuf.at[slot, u], q_recv.at[index])

        @pl.when(jnp.logical_and(layer > 0, field(code, 4) != x))
        def _():
            wait_for(fin.at[slot, u], f_recv.at[index])

        carried = stack_heads(fin[slot, u]).astype(jnp.float32)
        carried = jnp.where(layer == 0, 0.0, carried)
        mixed = (stack_heads(qbuf[slot, u]).astype(jnp.float32) + carried).astype(jnp.bfloat16)
        scores = merge(dot(mixed, kcat[slot], NT))
        mask = bias[field(code, 0) // KVH]
        scores = scores + jnp.concatenate([mask] * G, axis=0)
        lifted = jnp.exp2((scores - jnp.max(scores, axis=1, keepdims=True)) * EXP2_SCALE)
        weights = lifted * (1.0 / jnp.sum(lifted, axis=1, keepdims=True))
        wide = split(weights)
        out = side_by_side(dot(wide, vcat[slot], NN).astype(jnp.bfloat16))
        mixbuf[slot, u], wbuf[slot, u], pbuf[slot, u], obuf[slot, u] = mixed, weights, wide, out
        pass_on(obuf, fin, f_send, f_recv, code, index, True, start)
        deliver(obuf, att_hbm, code, index, 0, start, start)

        @pl.when(jnp.logical_and(layer < LAYERS - 1, field(code, 2) == x))
        def _():
            fin[field(code, 3), u] = out

    def backward_task(slot, u, code):
        index = slot * NU + u
        layer = field(code, 1)

        @pl.when(jnp.logical_or(layer == LAYERS - 1, field(code, 2) != x))
        def _():
            wait_for(gin.at[slot, u], b_recv.at[index])

        grad = stack_heads(gin[slot, u])
        weights = wbuf[slot, u]
        weight_grad = merge(dot(grad, vcat[slot], NT))
        row_dot = jnp.sum(weights * weight_grad, axis=1, keepdims=True)
        wide = split(weights * (weight_grad - row_dot) * SCALE)
        out = side_by_side(dot(wide, kcat[slot], NN).astype(jnp.bfloat16))
        dqbuf[slot, u] = out
        pass_on(dqbuf, gin, b_send, b_recv, code, index, False, start)
        deliver(dqbuf, qg_hbm, code, index, 1, start, start)

        @pl.when(jnp.logical_and(layer > 0, field(code, 4) == x))
        def _():
            gin[field(code, 5), u] = out

        dkt[slot] += dot(mixbuf[slot, u], wide, TN)
        dvt[slot] += dot(grad, pbuf[slot, u], TN)

        @pl.when(jnp.logical_and(u == NU - 1, jnp.logical_not(first_shard)))
        def _():
            part_send[slot, 0] = dkt[slot, :, :TOK].astype(jnp.bfloat16)
            part_send[slot, 1] = dvt[slot, :, :TOK].astype(jnp.bfloat16)
            part_copy(slot).start()

    def part_copy(slot):
        return pltpu.make_async_remote_copy(
            src_ref=part_send.at[slot],
            dst_ref=part_recv.at[slot],
            send_sem=part_send_sem.at[slot],
            recv_sem=part_recv_sem.at[slot],
            device_id=(x, jnp.maximum(c - 1, 0)),
            device_id_type=MESH,
        )

    @pl.loop(0, STEPS)
    def _(t):
        task = task_code(t)
        slot, u = lax.rem(task // 4, SLOTS), lax.rem(task, 4)
        code = choose(slot, codes)

        @pl.when(task < 16)
        def _():
            forward_task(slot, u, code)

        @pl.when(task >= 16)
        def _():
            backward_task(slot, u, code)

    def kv_deliver(slot, which, act, local):
        group, layer = field(codes[slot], 0), field(codes[slot], 1)
        src, dst = kvout.at[slot, which], kv_columns((kg_hbm, vg_hbm)[which], group)

        @pl.when(layer != x)
        def _():
            act(move(src, dst, home_send.at[2 + which, slot], home_recv.at[2 + which], layer))

        if local is not None:

            @pl.when(layer == x)
            def _():
                local(pltpu.make_async_copy(src, dst, home_recv.at[2 + which]))

    @pl.loop(0, SLOTS)
    def _(i):
        slot = choose(i, [choose(x, [last_slots(s)[j] for s in range(LAYERS)]) for j in range(SLOTS)])

        @pl.when(jnp.logical_not(last_shard))
        def _():
            wait_for(part_recv.at[slot], part_recv_sem.at[slot])

        for which, acc in enumerate((dkt, dvt)):
            extra = jnp.where(last_shard, 0.0, part_recv[slot, which].astype(jnp.float32))
            kvout[slot, which] = (acc[slot, :, TOK:] + extra).T.astype(jnp.bfloat16)
        code = choose(slot, codes)
        group, layer = field(code, 0), field(code, 1)
        for which, dst in enumerate((kg_hbm, vg_hbm)):
            src, dst = kvout.at[slot, which], kv_columns(dst, group)

            @pl.when(layer != x)
            def _():
                move(src, dst, home_send.at[2 + which, slot], home_recv.at[2 + which], layer).start()

            @pl.when(layer == x)
            def _():
                pltpu.make_async_copy(src, dst, home_recv.at[2 + which]).start()

    for g in order:
        for which in range(2):
            kv_move(g, which).wait_send()
        for u in range(NU):
            q_move(g, u).wait_send()

    for slot in range(SLOTS):

        @pl.when(jnp.logical_not(last_shard))
        def _():
            for which in range(2):
                halo(slot, which).wait_send()

        @pl.when(jnp.logical_not(first_shard))
        def _():
            part_copy(slot).wait_send()

        for u in range(NU):
            index = slot * NU + u
            pass_on(obuf, fin, f_send, f_recv, codes[slot], index, True, wait_send)
            pass_on(dqbuf, gin, b_send, b_recv, codes[slot], index, False, wait_send)
            deliver(obuf, att_hbm, codes[slot], index, 0, wait_send, None)
            deliver(dqbuf, qg_hbm, codes[slot], index, 1, wait_send, None)
        for which in range(2):
            kv_deliver(slot, which, wait_send, None)
    for kind, dst in enumerate((att_hbm, qg_hbm, kg_hbm, vg_hbm)):
        wait_for(dst, home_recv.at[kind])


def last_slots(section):
    ends = {}
    for t, task in enumerate(ORDER[section]):
        if task >= 16:
            ends[task // 4 % SLOTS] = t
    return sorted(ends, key=ends.get)


def settle(*refs):
    copies = [pltpu.make_async_copy(refs[i], refs[4 + i], refs[8].at[i]) for i in range(4)]
    for copy in copies:
        copy.start()
    for copy in copies:
        copy.wait()


def shards(query_in, key_in, value_in, doc_ids, out_grad):
    shards_n = lax.axis_size("ctx")
    bf16, f32 = jnp.bfloat16, jnp.float32
    feat, kv = HEADS * HD, KVH * HD
    hbm = pl.BlockSpec(memory_space=pl.ANY)
    dma = pltpu.SemaphoreType.DMA
    att, qg, kg, vg = pl.pallas_call(
        functools.partial(kernel, shards_n),
        out_shape=(
            pltpu.VMEM((MB, TOK, feat), bf16),
            pltpu.VMEM((MB, TOK, feat), bf16),
            pltpu.VMEM((MB, TOK, kv), bf16),
            pltpu.VMEM((MB, TOK, kv), bf16),
        ),
        in_specs=[hbm] * 5,
        out_specs=[pl.BlockSpec(memory_space=pltpu.VMEM)] * 4,
        scratch_shapes=[
            pltpu.VMEM((SLOTS, NU, TOK, COLS), bf16),
            pltpu.VMEM((SLOTS, NU, TOK, COLS), bf16),
            pltpu.VMEM((SLOTS, NU, TOK, COLS), bf16),
            pltpu.VMEM((SLOTS, NU, TOK, COLS), bf16),
            pltpu.VMEM((SLOTS, NU, TOK, COLS), bf16),
            pltpu.VMEM((SLOTS, NU, ROWS, HD), bf16),
            pltpu.VMEM((SLOTS, NU, ROWS, TOK), f32),
            pltpu.VMEM((SLOTS, NU, ROWS, 2 * TOK), bf16),
            pltpu.VMEM((SLOTS, 2 * TOK, HD), bf16),
            pltpu.VMEM((SLOTS, 2 * TOK, HD), bf16),
            pltpu.VMEM((MB, TOK, TOK), f32),
            pltpu.VMEM((MB, TOK), jnp.int32),
            pltpu.VMEM((MB, TOK), jnp.int32),
            pltpu.VMEM((SLOTS, HD, 2 * TOK), f32),
            pltpu.VMEM((SLOTS, HD, 2 * TOK), f32),
            pltpu.VMEM((SLOTS, 2, HD, TOK), bf16),
            pltpu.VMEM((SLOTS, 2, HD, TOK), bf16),
            pltpu.VMEM((SLOTS, 2, TOK, HD), bf16),
            dma((2,)),
            dma((NGRP * NU,)),
            dma((SLOTS * NU,)),
            dma((2 * NGRP,)),
            dma((2 * SLOTS,)),
            dma((2 * SLOTS,)),
            dma((2 * SLOTS,)),
            dma((SLOTS * NU,)),
            dma((SLOTS * NU,)),
            dma((SLOTS * NU,)),
            dma((SLOTS * NU,)),
            dma((SLOTS,)),
            dma((SLOTS,)),
            dma((4, SLOTS * NU)),
            dma((4,)),
        ],
        compiler_params=pltpu.CompilerParams(
            collective_id=0, has_side_effects=True, vmem_limit_bytes=32 * 1024 * 1024
        ),
        cost_estimate=pl.CostEstimate(flops=2_000_000_000, bytes_accessed=5_000_000, transcendentals=600_000),
    )(*[pltpu.with_memory_space_constraint(a, pltpu.HBM) for a in (query_in[0], key_in[0], value_in[0], doc_ids, out_grad)])
    att, qg, kg, vg = pl.pallas_call(
        settle,
        out_shape=[jax.ShapeDtypeStruct(a.shape, a.dtype) for a in (att, qg, kg, vg)],
        in_specs=[hbm] * 4,
        out_specs=[hbm] * 4,
        scratch_shapes=[dma((4,))],
        compiler_params=pltpu.CompilerParams(vmem_limit_bytes=1 * 1024 * 1024),
    )(att, qg, kg, vg)
    return (att[None], qg[None], kg[None], vg[None])


def solution(mesh):
    split = P("section", None, "ctx", None)
    return jax.shard_map(
        shards,
        mesh=mesh,
        in_specs=(split, split, split, P(), P(None, "ctx", None)),
        out_specs=(split, split, split, split),
        check_vma=False,
    )
```

```python
import functools
import math

import jax
import jax.numpy as jnp
from jax import lax
from jax.experimental import pallas as pl
from jax.experimental.pallas import tpu as pltpu
from jax.sharding import PartitionSpec as P

HD = 128
GROUP = 8
KVH = 2
HEADS = GROUP * KVH
MB = 2
TOK = 128
LAYERS = 4
DIRECT = 1
ROW = 16
FAR = LAYERS
SLOTS = LAYERS + 1
NGRP = MB * KVH
G = 4
NU = GROUP // G
COLS = G * HD
ROWS = G * TOK
MESH = pl.DeviceIdType.MESH
SCALE = 1.0 / math.sqrt(HD)
EXP2_SCALE = math.log2(math.e) / math.sqrt(HD)
NT = (((1,), (1,)), ((), ()))
NN = (((1,), (0,)), ((), ()))
TN = (((0,), (0,)), ((), ()))

def dot(a, b, dims):
    return lax.dot_general(a, b, dims, preferred_element_type=jnp.float32)


def stack_heads(x):
    return jnp.concatenate([x[:, h * HD : (h + 1) * HD] for h in range(G)], axis=0)


def side_by_side(x):
    return jnp.concatenate([x[h * TOK : (h + 1) * TOK] for h in range(G)], axis=1)


def kernel(
    shards_n,
    q_hbm,
    k_hbm,
    v_hbm,
    ids_hbm,
    og_hbm,
    att_hbm,
    qg_hbm,
    kg_hbm,
    vg_hbm,
    qbuf,
    gin,
    far_in,
    obuf,
    dqbuf,
    mixbuf,
    wbuf,
    pbuf,
    kcat,
    vcat,
    bias,
    own_ids,
    prev_ids,
    dkt,
    dvt,
    part_send,
    part_recv,
    kvout,
    ids_sem,
    q_send,
    q_recv,
    kv_send,
    kv_recv,
    halo_send,
    halo_recv,
    b_recv,
    part_send_sem,
    part_recv_sem,
    home_send,
    home_recv,
    near_send,
    near_recv,
    far_send,
    far_recv,
    direct_send,
):
    x = lax.axis_index("section")
    c = lax.axis_index("ctx")
    first_shard = c == 0
    last_shard = c == shards_n - 1
    edge = jnp.logical_and(lax.rem(c, ROW) == ROW - 1, jnp.logical_not(last_shard))
    after_edge = jnp.logical_and(lax.rem(c, ROW) == 0, jnp.logical_not(first_shard))
    after, before, opposite = (lax.rem(x + d, LAYERS) for d in (1, 3, 2))

    barrier = pltpu.get_barrier_semaphore()
    for d in range(1, LAYERS):
        pl.semaphore_signal(barrier, inc=1, device_id=(lax.rem(x + d, LAYERS), c), device_id_type=MESH)

    @pl.when(jnp.logical_not(first_shard))
    def _():
        pl.semaphore_signal(barrier, inc=1, device_id=(x, jnp.maximum(c - 1, 0)), device_id_type=MESH)

    @pl.when(after_edge)
    def _():
        for section in (after, before, opposite):
            pl.semaphore_signal(
                barrier, inc=1, device_id=(section, jnp.maximum(c - 1, 0)), device_id_type=MESH
            )

    def move(src, dst, send_sem, recv_sem, section):
        return pltpu.make_async_remote_copy(
            src_ref=src,
            dst_ref=dst,
            send_sem=send_sem,
            recv_sem=recv_sem,
            device_id=(section, c),
            device_id_type=MESH,
        )

    def wait_for(ref, sem):
        pltpu.make_async_copy(ref, ref, sem).wait()

    def columns(ref, group, unit):
        m, n = group // KVH, lax.rem(group, KVH)
        return ref.at[m, :, pl.ds(pl.multiple_of(n * GROUP * HD + unit * COLS, COLS), COLS)]

    def kv_columns(ref, group):
        m, n = group // KVH, lax.rem(group, KVH)
        return ref.at[m, :, pl.ds(pl.multiple_of(n * HD, HD), HD)]

    own_at = pl.multiple_of(c * TOK, TOK)
    prev_at = pl.multiple_of(jnp.maximum(c - 1, 0) * TOK, TOK)
    own_copy = pltpu.make_async_copy(ids_hbm.at[:, pl.ds(own_at, TOK)], own_ids, ids_sem.at[0])
    prev_copy = pltpu.make_async_copy(ids_hbm.at[:, pl.ds(prev_at, TOK)], prev_ids, ids_sem.at[1])
    own_copy.start()
    prev_copy.start()

    for which, (src, dst) in enumerate(((k_hbm, kcat), (v_hbm, vcat))):
        pltpu.make_async_copy(kv_columns(src, x), dst.at[x, pl.ds(TOK, TOK)], kv_recv.at[2 * x + which]).start()
        pltpu.make_async_copy(
            kv_columns(src, opposite), dst.at[FAR, pl.ds(TOK, TOK)], kv_recv.at[2 * FAR + which]
        ).start()
    for u in range(NU):
        pltpu.make_async_copy(columns(q_hbm, x, u), qbuf.at[x, u], q_recv.at[x * NU + u]).start()
        pltpu.make_async_copy(columns(q_hbm, opposite, u), qbuf.at[FAR, u], q_recv.at[FAR * NU + u]).start()
        pltpu.make_async_copy(columns(og_hbm, x, u), gin.at[u], b_recv.at[u]).start()

        @pl.when(x == LAYERS - 1)
        def _():
            pltpu.make_async_copy(columns(og_hbm, opposite, u), far_in.at[1, u], far_recv.at[1, u]).start()

    dkt[...] = jnp.zeros_like(dkt)
    dvt[...] = jnp.zeros_like(dvt)

    @pl.when(first_shard)
    def _():
        for slot in range(SLOTS):
            kcat[slot, :TOK] = jnp.zeros((TOK, HD), jnp.bfloat16)
            vcat[slot, :TOK] = jnp.zeros((TOK, HD), jnp.bfloat16)

    heard = jnp.where(last_shard, LAYERS - 1, jnp.where(edge, 2 * LAYERS - 1, LAYERS))
    pl.semaphore_wait(barrier, heard)

    others = (opposite, after, before)

    def kv_move(g, which):
        src, dst = ((k_hbm, kcat), (v_hbm, vcat))[which]
        return move(
            kv_columns(src, g),
            dst.at[x, pl.ds(TOK, TOK)],
            kv_send.at[2 * g + which],
            kv_recv.at[2 * x + which],
            g,
        )

    def q_move(g, u):
        return move(columns(q_hbm, g, u), qbuf.at[x, u], q_send.at[g * NU + u], q_recv.at[x * NU + u], g)

    def edge_move(g, which):
        src, dst = ((k_hbm, kcat), (v_hbm, vcat))[which]
        return pltpu.make_async_remote_copy(
            src_ref=kv_columns(src, g),
            dst_ref=dst.at[x, pl.ds(0, TOK)],
            send_sem=halo_send.at[2 * g + which],
            recv_sem=halo_recv.at[2 * x + which],
            device_id=(g, jnp.minimum(c + 1, shards_n - 1)),
            device_id_type=MESH,
        )

    @pl.when(edge)
    def _():
        for g in others:
            for which in range(2):
                edge_move(g, which).start()

    for g in others:
        for which in range(2):
            kv_move(g, which).start()
    for u in range(NU):
        for g in others:
            q_move(g, u).start()

    row = lax.broadcasted_iota(jnp.int32, (TOK, TOK), 0)
    col = lax.broadcasted_iota(jnp.int32, (TOK, TOK), 1)
    own_copy.wait()
    prev_copy.wait()
    for m in range(MB):
        own_row = jnp.broadcast_to(own_ids[m : m + 1, :], (TOK, TOK)).astype(jnp.float32)
        prev_row = jnp.broadcast_to(prev_ids[m : m + 1, :], (TOK, TOK)).astype(jnp.float32)
        prev_row = jnp.where(first_shard, -1.0, prev_row)
        seen = jnp.where(col <= row, own_row, prev_row)
        bias[m] = jnp.where(seen == own_row.T, 0.0, -1e30)

    def hands_on(slot):
        if slot == FAR:
            return True
        return jnp.logical_or(jnp.logical_not(edge), slot == x)

    def halo(slot, which):
        dst = (kcat, vcat)[which]
        return pltpu.make_async_remote_copy(
            src_ref=dst.at[slot, pl.ds(TOK, TOK)],
            dst_ref=dst.at[slot, pl.ds(0, TOK)],
            send_sem=halo_send.at[2 * slot + which],
            recv_sem=halo_recv.at[2 * slot + which],
            device_id=(x, jnp.minimum(c + 1, shards_n - 1)),
            device_id_type=MESH,
        )

    for slot in (FAR, *range(LAYERS)):
        for which, dst in enumerate((kcat, vcat)):
            wait_for(dst.at[slot, pl.ds(TOK, TOK)], kv_recv.at[2 * slot + which])

        @pl.when(jnp.logical_and(jnp.logical_not(last_shard), hands_on(slot)))
        def _():
            for which in range(2):
                halo(slot, which).start()

    def tri():
        rows = lax.broadcasted_iota(jnp.int32, (ROWS, TOK), 0)
        cols = lax.broadcasted_iota(jnp.int32, (ROWS, TOK), 1)
        return cols <= lax.rem(rows, TOK)

    def split(weights):
        own = tri()
        prev_half = jnp.where(own, 0.0, weights).astype(jnp.bfloat16)
        own_half = jnp.where(own, weights, 0.0).astype(jnp.bfloat16)
        return jnp.concatenate([prev_half, own_half], axis=1)

    def merge(wide):
        return jnp.where(tri(), wide[:, TOK:], wide[:, :TOK])

    results = ((obuf, att_hbm), (dqbuf, qg_hbm))

    def home_move(kind, u):
        buf, dst = results[kind]
        layer = (before, after)[kind]
        return move(buf.at[layer, u], columns(dst, x, u), home_send.at[kind, u], home_recv.at[kind], layer)

    def near_move(kind, u):
        buf, dst = results[kind]
        layer = (after, before)[kind]
        return move(buf.at[layer, u], columns(dst, x, u), near_send.at[kind, u], near_recv.at[kind, u], layer)

    def far_move(kind, u):
        dst = results[kind][1]
        group, section = ((before, after), (after, before))[kind]
        return move(
            columns(dst, group, u), far_in.at[kind, u], far_send.at[kind, u], far_recv.at[kind, u], section
        )

    def direct_move(u):
        return move(
            dqbuf.at[before, u], far_in.at[1, u], direct_send.at[u], far_recv.at[1, u], opposite
        )

    more = (x < LAYERS - 1, x > 0)

    def pass_on(kind, u):
        group = (before, after)[kind]
        wait_for(columns(results[kind][1], group, u), near_recv.at[kind, u])

        @pl.when(jnp.logical_and(more[kind], u < (NU, DIRECT)[kind]))
        def _():
            far_move(kind, u).start()

    def keep(kind, slot, group, u):
        buf, dst = results[kind]
        pltpu.make_async_copy(buf.at[slot, u], columns(dst, group, u), home_recv.at[kind]).start()

    def forward_task(slot, u, group, carried):
        wait_for(qbuf.at[slot, u], q_recv.at[slot * NU + u])

        @pl.when(jnp.logical_and(u == 0, jnp.logical_not(first_shard)))
        def _():
            for which, dst in enumerate((kcat, vcat)):
                wait_for(dst.at[slot, pl.ds(0, TOK)], halo_recv.at[2 * slot + which])

        mixed = (stack_heads(qbuf[slot, u]).astype(jnp.float32) + carried).astype(jnp.bfloat16)
        scores = merge(dot(mixed, kcat[slot], NT))
        mask = bias[group // KVH]
        scores = scores + jnp.concatenate([mask] * G, axis=0)
        lifted = jnp.exp2((scores - jnp.max(scores, axis=1, keepdims=True)) * EXP2_SCALE)
        weights = lifted * (1.0 / jnp.sum(lifted, axis=1, keepdims=True))
        wide = split(weights)
        out = side_by_side(dot(wide, vcat[slot], NN).astype(jnp.bfloat16))
        mixbuf[slot, u], wbuf[slot, u], pbuf[slot, u], obuf[slot, u] = mixed, weights, wide, out

    def backward_task(slot, u, grad, sums):
        grad = stack_heads(grad)
        weights = wbuf[slot, u]
        weight_grad = merge(dot(grad, vcat[slot], NT))
        row_dot = jnp.sum(weights * weight_grad, axis=1, keepdims=True)
        wide = split(weights * (weight_grad - row_dot) * SCALE)
        dqbuf[slot, u] = side_by_side(dot(wide, kcat[slot], NN).astype(jnp.bfloat16))

        @pl.when(sums)
        def _():
            dkt[slot] += dot(mixbuf[slot, u], wide, TN)
            dvt[slot] += dot(grad, pbuf[slot, u], TN)

            @pl.when(jnp.logical_and(u == NU - 1, jnp.logical_not(first_shard)))
            def _():
                part_send[slot, 0] = dkt[slot, :, :TOK].astype(jnp.bfloat16)
                part_send[slot, 1] = dvt[slot, :, :TOK].astype(jnp.bfloat16)
                part_copy(slot).start()

    def part_copy(slot):
        return pltpu.make_async_remote_copy(
            src_ref=part_send.at[slot],
            dst_ref=part_recv.at[slot],
            send_sem=part_send_sem.at[slot],
            recv_sem=part_recv_sem.at[slot],
            device_id=(x, jnp.maximum(c - 1, 0)),
            device_id_type=MESH,
        )

    def forward_own(u):
        @pl.loop(0, LAYERS)
        def _(layer):
            carried = stack_heads(obuf[jnp.maximum(layer - 1, 0), u]).astype(jnp.float32)
            forward_task(layer, u, x, jnp.where(layer == 0, 0.0, carried))

            @pl.when(layer == after)
            def _():
                near_move(0, u).start()

        keep(0, x, x, u)

    def backward_own(u):
        @pl.loop(0, LAYERS)
        def _(i):
            layer = LAYERS - 1 - i
            below = dqbuf[jnp.minimum(layer + 1, LAYERS - 1), u]
            backward_task(layer, u, jnp.where(layer == LAYERS - 1, gin[u], below), layer != opposite)

            @pl.when(layer == before)
            def _():
                near_move(1, u).start()

                @pl.when(jnp.logical_and(u >= DIRECT, opposite < LAYERS - 1))
                def _():
                    direct_move(u).start()

        keep(1, x, x, u)

    def kv_sums(slot):
        @pl.when(jnp.logical_not(last_shard))
        def _():
            wait_for(part_recv.at[slot], part_recv_sem.at[slot])

        for which, acc in enumerate((dkt, dvt)):
            extra = jnp.where(last_shard, 0.0, part_recv[slot, which].astype(jnp.float32))
            kvout[slot, which] = (acc[slot, :, TOK:] + extra).T.astype(jnp.bfloat16)

    def kv_home(layer, which):
        return move(
            kvout.at[layer, which],
            kv_columns((kg_hbm, vg_hbm)[which], x),
            home_send.at[2 + which, layer],
            home_recv.at[2 + which],
            layer,
        )

    def kv_keep(slot, group):
        for which, dst in enumerate((kg_hbm, vg_hbm)):
            pltpu.make_async_copy(kvout.at[slot, which], kv_columns(dst, group), home_recv.at[2 + which]).start()

    def kv_own():
        @pl.loop(0, LAYERS)
        def _(i):
            layer = LAYERS - 1 - i

            @pl.when(layer != opposite)
            def _():
                kv_sums(layer)

                @pl.when(layer != x)
                def _():
                    for which in range(2):
                        kv_home(layer, which).start()

                @pl.when(layer == x)
                def _():
                    kv_keep(layer, x)

    def forward_far(u):
        @pl.when(x > 0)
        def _():
            wait_for(far_in.at[0, u], far_recv.at[0, u])

        carried = stack_heads(far_in[0, u]).astype(jnp.float32)
        forward_task(FAR, u, opposite, jnp.where(x == 0, 0.0, carried))
        keep(0, FAR, opposite, u)

    def backward_far(u):
        wait_for(far_in.at[1, u], far_recv.at[1, u])
        backward_task(FAR, u, far_in[1, u], True)
        keep(1, FAR, opposite, u)

    for u in range(NU):
        wait_for(gin.at[u], b_recv.at[u])

    forward_own(0)
    backward_own(0)
    home_move(0, 0).start()
    forward_own(1)
    pass_on(0, 0)
    backward_own(1)
    pass_on(0, 1)
    home_move(1, 0).start()
    pass_on(1, 0)
    home_move(1, 1).start()
    forward_far(0)
    forward_far(1)
    home_move(0, 1).start()
    backward_far(0)
    kv_own()
    backward_far(1)
    pass_on(1, 1)
    kv_sums(FAR)
    kv_keep(FAR, opposite)

    @pl.when(edge)
    def _():
        for g in others:
            for which in range(2):
                edge_move(g, which).wait_send()

    for other in others:
        for which in range(2):
            kv_move(other, which).wait_send()
        for u in range(NU):
            q_move(other, u).wait_send()
    for other in (after, before):
        for which in range(2):
            kv_home(other, which).wait_send()
    for u in range(NU):
        for kind in range(2):
            home_move(kind, u).wait_send()
            near_move(kind, u).wait_send()

            if kind == 0 or u < DIRECT:

                @pl.when(more[kind])
                def _():
                    far_move(kind, u).wait_send()

        if u >= DIRECT:

            @pl.when(opposite < LAYERS - 1)
            def _():
                direct_move(u).wait_send()

    for slot in range(SLOTS):

        @pl.when(jnp.logical_and(jnp.logical_not(last_shard), hands_on(slot)))
        def _():
            for which in range(2):
                halo(slot, which).wait_send()

        @pl.when(jnp.logical_and(slot != opposite, jnp.logical_not(first_shard)))
        def _():
            part_copy(slot).wait_send()

    kept = pl.ds(0, TOK * (LAYERS - 1) // LAYERS)
    for kind, dst in enumerate((att_hbm, qg_hbm)):
        wait_for(dst.at[:, kept], home_recv.at[kind])
    for which, dst in enumerate((kg_hbm, vg_hbm)):
        wait_for(dst, home_recv.at[2 + which])


def settle(*refs):
    copies = [pltpu.make_async_copy(refs[i], refs[4 + i], refs[8].at[i]) for i in range(4)]
    for copy in copies:
        copy.start()
    for copy in copies:
        copy.wait()


def shards(query_in, key_in, value_in, doc_ids, out_grad):
    shards_n = lax.axis_size("ctx")
    bf16, f32 = jnp.bfloat16, jnp.float32
    feat, kv = HEADS * HD, KVH * HD
    hbm = pl.BlockSpec(memory_space=pl.ANY)
    dma = pltpu.SemaphoreType.DMA
    att, qg, kg, vg = pl.pallas_call(
        functools.partial(kernel, shards_n),
        out_shape=(
            pltpu.VMEM((MB, TOK, feat), bf16),
            pltpu.VMEM((MB, TOK, feat), bf16),
            pltpu.VMEM((MB, TOK, kv), bf16),
            pltpu.VMEM((MB, TOK, kv), bf16),
        ),
        in_specs=[hbm] * 5,
        out_specs=[pl.BlockSpec(memory_space=pltpu.VMEM)] * 4,
        scratch_shapes=[
            pltpu.VMEM((SLOTS, NU, TOK, COLS), bf16),
            pltpu.VMEM((NU, TOK, COLS), bf16),
            pltpu.VMEM((2, NU, TOK, COLS), bf16),
            pltpu.VMEM((SLOTS, NU, TOK, COLS), bf16),
            pltpu.VMEM((SLOTS, NU, TOK, COLS), bf16),
            pltpu.VMEM((SLOTS, NU, ROWS, HD), bf16),
            pltpu.VMEM((SLOTS, NU, ROWS, TOK), f32),
            pltpu.VMEM((SLOTS, NU, ROWS, 2 * TOK), bf16),
            pltpu.VMEM((SLOTS, 2 * TOK, HD), bf16),
            pltpu.VMEM((SLOTS, 2 * TOK, HD), bf16),
            pltpu.VMEM((MB, TOK, TOK), f32),
            pltpu.VMEM((MB, TOK), jnp.int32),
            pltpu.VMEM((MB, TOK), jnp.int32),
            pltpu.VMEM((SLOTS, HD, 2 * TOK), f32),
            pltpu.VMEM((SLOTS, HD, 2 * TOK), f32),
            pltpu.VMEM((SLOTS, 2, HD, TOK), bf16),
            pltpu.VMEM((SLOTS, 2, HD, TOK), bf16),
            pltpu.VMEM((SLOTS, 2, TOK, HD), bf16),
            dma((2,)),
            dma((NGRP * NU,)),
            dma((SLOTS * NU,)),
            dma((2 * NGRP,)),
            dma((2 * SLOTS,)),
            dma((2 * SLOTS,)),
            dma((2 * SLOTS,)),
            dma((NU,)),
            dma((SLOTS,)),
            dma((SLOTS,)),
            dma((4, LAYERS * NU)),
            dma((4,)),
            dma((2, NU)),
            dma((2, NU)),
            dma((2, NU)),
            dma((2, NU)),
            dma((NU,)),
        ],
        compiler_params=pltpu.CompilerParams(
            collective_id=0, has_side_effects=True, vmem_limit_bytes=32 * 1024 * 1024
        ),
        cost_estimate=pl.CostEstimate(flops=2_000_000_000, bytes_accessed=5_000_000, transcendentals=600_000),
    )(*[pltpu.with_memory_space_constraint(a, pltpu.HBM) for a in (query_in[0], key_in[0], value_in[0], doc_ids, out_grad)])
    att, qg, kg, vg = pl.pallas_call(
        settle,
        out_shape=[jax.ShapeDtypeStruct(a.shape, a.dtype) for a in (att, qg, kg, vg)],
        in_specs=[hbm] * 4,
        out_specs=[hbm] * 4,
        scratch_shapes=[dma((4,))],
        compiler_params=pltpu.CompilerParams(vmem_limit_bytes=1 * 1024 * 1024),
    )(att, qg, kg, vg)
    return (att[None], qg[None], kg[None], vg[None])


def solution(mesh):
    split = P("section", None, "ctx", None)
    return jax.shard_map(
        shards,
        mesh=mesh,
        in_specs=(split, split, split, P(), P(None, "ctx", None)),
        out_specs=(split, split, split, split),
        check_vma=False,
    )
```

```python
import functools
import math

import jax
import jax.numpy as jnp
from jax import lax
from jax.experimental import pallas as pl
from jax.experimental.pallas import tpu as pltpu
from jax.sharding import PartitionSpec as P

HD = 128
GROUP = 8
KVH = 2
HEADS = GROUP * KVH
MB = 2
TOK = 128
LAYERS = 4
DIRECT = 1
ROW = 16
FAR = LAYERS
SLOTS = LAYERS + 1
NGRP = MB * KVH
G = 4
NU = GROUP // G
COLS = G * HD
ROWS = G * TOK
MESH = pl.DeviceIdType.MESH
SCALE = 1.0 / math.sqrt(HD)
EXP2_SCALE = math.log2(math.e) / math.sqrt(HD)
NT = (((1,), (1,)), ((), ()))
NN = (((1,), (0,)), ((), ()))
TN = (((0,), (0,)), ((), ()))

def dot(a, b, dims):
    return lax.dot_general(a, b, dims, preferred_element_type=jnp.float32)


def stack_heads(x):
    return jnp.concatenate([x[:, h * HD : (h + 1) * HD] for h in range(G)], axis=0)


def side_by_side(x):
    return jnp.concatenate([x[h * TOK : (h + 1) * TOK] for h in range(G)], axis=1)


def kernel(
    shards_n,
    q_hbm,
    k_hbm,
    v_hbm,
    ids_hbm,
    og_hbm,
    att_hbm,
    qg_hbm,
    kg_hbm,
    vg_hbm,
    qbuf,
    gin,
    far_in,
    obuf,
    dqbuf,
    mixbuf,
    wbuf,
    pbuf,
    kcat,
    vcat,
    bias,
    own_ids,
    prev_ids,
    dkt,
    dvt,
    part_send,
    part_recv,
    kvout,
    ids_sem,
    q_send,
    q_recv,
    kv_send,
    kv_recv,
    halo_send,
    halo_recv,
    b_recv,
    part_send_sem,
    part_recv_sem,
    home_send,
    home_recv,
    near_send,
    near_recv,
    far_send,
    far_recv,
    direct_send,
):
    x = lax.axis_index("section")
    c = lax.axis_index("ctx")
    first_shard = c == 0
    last_shard = c == shards_n - 1
    edge = jnp.logical_and(lax.rem(c, ROW) == ROW - 1, jnp.logical_not(last_shard))
    after_edge = jnp.logical_and(lax.rem(c, ROW) == 0, jnp.logical_not(first_shard))
    after, before, opposite = (lax.rem(x + d, LAYERS) for d in (1, 3, 2))

    barrier = pltpu.get_barrier_semaphore()
    for d in range(1, LAYERS):
        pl.semaphore_signal(barrier, inc=1, device_id=(lax.rem(x + d, LAYERS), c), device_id_type=MESH)

    @pl.when(jnp.logical_not(first_shard))
    def _():
        pl.semaphore_signal(barrier, inc=1, device_id=(x, jnp.maximum(c - 1, 0)), device_id_type=MESH)

    @pl.when(after_edge)
    def _():
        for section in (after, before, opposite):
            pl.semaphore_signal(
                barrier, inc=1, device_id=(section, jnp.maximum(c - 1, 0)), device_id_type=MESH
            )

    def move(src, dst, send_sem, recv_sem, section):
        return pltpu.make_async_remote_copy(
            src_ref=src,
            dst_ref=dst,
            send_sem=send_sem,
            recv_sem=recv_sem,
            device_id=(section, c),
            device_id_type=MESH,
        )

    def wait_for(ref, sem):
        pltpu.make_async_copy(ref, ref, sem).wait()

    def columns(ref, group, unit):
        m, n = group // KVH, lax.rem(group, KVH)
        return ref.at[m, :, pl.ds(pl.multiple_of(n * GROUP * HD + unit * COLS, COLS), COLS)]

    def kv_columns(ref, group):
        m, n = group // KVH, lax.rem(group, KVH)
        return ref.at[m, :, pl.ds(pl.multiple_of(n * HD, HD), HD)]

    own_at = pl.multiple_of(c * TOK, TOK)
    prev_at = pl.multiple_of(jnp.maximum(c - 1, 0) * TOK, TOK)
    own_copy = pltpu.make_async_copy(ids_hbm.at[:, pl.ds(own_at, TOK)], own_ids, ids_sem.at[0])
    prev_copy = pltpu.make_async_copy(ids_hbm.at[:, pl.ds(prev_at, TOK)], prev_ids, ids_sem.at[1])
    own_copy.start()
    prev_copy.start()

    for which, (src, dst) in enumerate(((k_hbm, kcat), (v_hbm, vcat))):
        pltpu.make_async_copy(kv_columns(src, x), dst.at[x, pl.ds(TOK, TOK)], kv_recv.at[2 * x + which]).start()
        pltpu.make_async_copy(
            kv_columns(src, opposite), dst.at[FAR, pl.ds(TOK, TOK)], kv_recv.at[2 * FAR + which]
        ).start()
    for u in range(NU):
        pltpu.make_async_copy(columns(q_hbm, x, u), qbuf.at[x, u], q_recv.at[x * NU + u]).start()
        pltpu.make_async_copy(columns(q_hbm, opposite, u), qbuf.at[FAR, u], q_recv.at[FAR * NU + u]).start()
        pltpu.make_async_copy(columns(og_hbm, x, u), gin.at[u], b_recv.at[u]).start()

        @pl.when(x == LAYERS - 1)
        def _():
            pltpu.make_async_copy(columns(og_hbm, opposite, u), far_in.at[1, u], far_recv.at[1, u]).start()

    dkt[...] = jnp.zeros_like(dkt)
    dvt[...] = jnp.zeros_like(dvt)

    @pl.when(first_shard)
    def _():
        for slot in range(SLOTS):
            kcat[slot, :TOK] = jnp.zeros((TOK, HD), jnp.bfloat16)
            vcat[slot, :TOK] = jnp.zeros((TOK, HD), jnp.bfloat16)

    heard = jnp.where(last_shard, LAYERS - 1, jnp.where(edge, 2 * LAYERS - 1, LAYERS))
    pl.semaphore_wait(barrier, heard)

    others = (opposite, after, before)

    def kv_move(g, which):
        src, dst = ((k_hbm, kcat), (v_hbm, vcat))[which]
        return move(
            kv_columns(src, g),
            dst.at[x, pl.ds(TOK, TOK)],
            kv_send.at[2 * g + which],
            kv_recv.at[2 * x + which],
            g,
        )

    def q_move(g, u):
        return move(columns(q_hbm, g, u), qbuf.at[x, u], q_send.at[g * NU + u], q_recv.at[x * NU + u], g)

    def edge_move(g, which):
        src, dst = ((k_hbm, kcat), (v_hbm, vcat))[which]
        return pltpu.make_async_remote_copy(
            src_ref=kv_columns(src, g),
            dst_ref=dst.at[x, pl.ds(0, TOK)],
            send_sem=halo_send.at[2 * g + which],
            recv_sem=halo_recv.at[2 * x + which],
            device_id=(g, jnp.minimum(c + 1, shards_n - 1)),
            device_id_type=MESH,
        )

    @pl.when(edge)
    def _():
        for g in others:
            for which in range(2):
                edge_move(g, which).start()

    for g in others:
        for which in range(2):
            kv_move(g, which).start()
    for u in range(NU):
        for g in others:
            q_move(g, u).start()

    row = lax.broadcasted_iota(jnp.int32, (TOK, TOK), 0)
    col = lax.broadcasted_iota(jnp.int32, (TOK, TOK), 1)
    own_copy.wait()
    prev_copy.wait()
    for m in range(MB):
        own_row = jnp.broadcast_to(own_ids[m : m + 1, :], (TOK, TOK)).astype(jnp.float32)
        prev_row = jnp.broadcast_to(prev_ids[m : m + 1, :], (TOK, TOK)).astype(jnp.float32)
        prev_row = jnp.where(first_shard, -1.0, prev_row)
        seen = jnp.where(col <= row, own_row, prev_row)
        bias[m] = jnp.where(seen == own_row.T, 0.0, -1e30)

    def hands_on(slot):
        if slot == FAR:
            return True
        return jnp.logical_or(jnp.logical_not(edge), slot == x)

    def halo(slot, which):
        dst = (kcat, vcat)[which]
        return pltpu.make_async_remote_copy(
            src_ref=dst.at[slot, pl.ds(TOK, TOK)],
            dst_ref=dst.at[slot, pl.ds(0, TOK)],
            send_sem=halo_send.at[2 * slot + which],
            recv_sem=halo_recv.at[2 * slot + which],
            device_id=(x, jnp.minimum(c + 1, shards_n - 1)),
            device_id_type=MESH,
        )

    for slot in (FAR, *range(LAYERS)):
        for which, dst in enumerate((kcat, vcat)):
            wait_for(dst.at[slot, pl.ds(TOK, TOK)], kv_recv.at[2 * slot + which])

        @pl.when(jnp.logical_and(jnp.logical_not(last_shard), hands_on(slot)))
        def _():
            for which in range(2):
                halo(slot, which).start()

    def tri():
        rows = lax.broadcasted_iota(jnp.int32, (ROWS, TOK), 0)
        cols = lax.broadcasted_iota(jnp.int32, (ROWS, TOK), 1)
        return cols <= lax.rem(rows, TOK)

    def split(weights):
        own = tri()
        prev_half = jnp.where(own, 0.0, weights).astype(jnp.bfloat16)
        own_half = jnp.where(own, weights, 0.0).astype(jnp.bfloat16)
        return jnp.concatenate([prev_half, own_half], axis=1)

    def merge(wide):
        return jnp.where(tri(), wide[:, TOK:], wide[:, :TOK])

    results = ((obuf, att_hbm), (dqbuf, qg_hbm))

    def home_move(kind, u):
        buf, dst = results[kind]
        layer = (before, after)[kind]
        return move(buf.at[layer, u], columns(dst, x, u), home_send.at[kind, u], home_recv.at[kind], layer)

    def near_move(kind, u):
        buf, dst = results[kind]
        layer = (after, before)[kind]
        return move(buf.at[layer, u], columns(dst, x, u), near_send.at[kind, u], near_recv.at[kind, u], layer)

    def far_move(kind, u):
        dst = results[kind][1]
        group, section = ((before, after), (after, before))[kind]
        return move(
            columns(dst, group, u), far_in.at[kind, u], far_send.at[kind, u], far_recv.at[kind, u], section
        )

    def direct_move(u):
        return move(
            dqbuf.at[before, u], far_in.at[1, u], direct_send.at[u], far_recv.at[1, u], opposite
        )

    more = (x < LAYERS - 1, x > 0)

    def pass_on(kind, u):
        group = (before, after)[kind]
        wait_for(columns(results[kind][1], group, u), near_recv.at[kind, u])

        @pl.when(jnp.logical_and(more[kind], u < (NU, DIRECT)[kind]))
        def _():
            far_move(kind, u).start()

    def keep(kind, slot, group, u):
        buf, dst = results[kind]
        pltpu.make_async_copy(buf.at[slot, u], columns(dst, group, u), home_recv.at[kind]).start()

    def forward_task(slot, u, group, carried):
        wait_for(qbuf.at[slot, u], q_recv.at[slot * NU + u])

        @pl.when(jnp.logical_and(u == 0, jnp.logical_not(first_shard)))
        def _():
            for which, dst in enumerate((kcat, vcat)):
                wait_for(dst.at[slot, pl.ds(0, TOK)], halo_recv.at[2 * slot + which])

        mixed = (stack_heads(qbuf[slot, u]).astype(jnp.float32) + carried).astype(jnp.bfloat16)
        scores = merge(dot(mixed, kcat[slot], NT))
        mask = bias[group // KVH]
        scores = scores + jnp.concatenate([mask] * G, axis=0)
        lifted = jnp.exp2((scores - jnp.max(scores, axis=1, keepdims=True)) * EXP2_SCALE)
        weights = lifted * (1.0 / jnp.sum(lifted, axis=1, keepdims=True))
        wide = split(weights)
        out = side_by_side(dot(wide, vcat[slot], NN).astype(jnp.bfloat16))
        mixbuf[slot, u], wbuf[slot, u], pbuf[slot, u], obuf[slot, u] = mixed, weights, wide, out

    def backward_task(slot, u, grad, sums):
        grad = stack_heads(grad)
        weights = wbuf[slot, u]
        weight_grad = merge(dot(grad, vcat[slot], NT))
        row_dot = jnp.sum(weights * weight_grad, axis=1, keepdims=True)
        wide = split(weights * (weight_grad - row_dot) * SCALE)
        dqbuf[slot, u] = side_by_side(dot(wide, kcat[slot], NN).astype(jnp.bfloat16))

        @pl.when(sums)
        def _():
            dkt[slot] += dot(mixbuf[slot, u], wide, TN)
            dvt[slot] += dot(grad, pbuf[slot, u], TN)

            @pl.when(jnp.logical_and(u == NU - 1, jnp.logical_not(first_shard)))
            def _():
                part_send[slot, 0] = dkt[slot, :, :TOK].astype(jnp.bfloat16)
                part_send[slot, 1] = dvt[slot, :, :TOK].astype(jnp.bfloat16)
                part_copy(slot).start()

    def part_copy(slot):
        return pltpu.make_async_remote_copy(
            src_ref=part_send.at[slot],
            dst_ref=part_recv.at[slot],
            send_sem=part_send_sem.at[slot],
            recv_sem=part_recv_sem.at[slot],
            device_id=(x, jnp.maximum(c - 1, 0)),
            device_id_type=MESH,
        )

    def forward_own(u):
        @pl.loop(0, LAYERS)
        def _(layer):
            carried = stack_heads(obuf[jnp.maximum(layer - 1, 0), u]).astype(jnp.float32)
            forward_task(layer, u, x, jnp.where(layer == 0, 0.0, carried))

            @pl.when(layer == after)
            def _():
                near_move(0, u).start()

        keep(0, x, x, u)

    def backward_own(u):
        @pl.loop(0, LAYERS)
        def _(i):
            layer = LAYERS - 1 - i
            below = dqbuf[jnp.minimum(layer + 1, LAYERS - 1), u]
            backward_task(layer, u, jnp.where(layer == LAYERS - 1, gin[u], below), layer != opposite)

            @pl.when(layer == before)
            def _():
                near_move(1, u).start()

                @pl.when(jnp.logical_and(u >= DIRECT, opposite < LAYERS - 1))
                def _():
                    direct_move(u).start()

        keep(1, x, x, u)

    def kv_sums(slot):
        @pl.when(jnp.logical_not(last_shard))
        def _():
            wait_for(part_recv.at[slot], part_recv_sem.at[slot])

        for which, acc in enumerate((dkt, dvt)):
            extra = jnp.where(last_shard, 0.0, part_recv[slot, which].astype(jnp.float32))
            kvout[slot, which] = (acc[slot, :, TOK:] + extra).T.astype(jnp.bfloat16)

    def kv_home(layer, which):
        return move(
            kvout.at[layer, which],
            kv_columns((kg_hbm, vg_hbm)[which], x),
            home_send.at[2 + which, layer],
            home_recv.at[2 + which],
            layer,
        )

    def kv_keep(slot, group):
        for which, dst in enumerate((kg_hbm, vg_hbm)):
            pltpu.make_async_copy(kvout.at[slot, which], kv_columns(dst, group), home_recv.at[2 + which]).start()

    def kv_own():
        @pl.loop(0, LAYERS)
        def _(i):
            layer = LAYERS - 1 - i

            @pl.when(layer != opposite)
            def _():
                kv_sums(layer)

                @pl.when(layer != x)
                def _():
                    for which in range(2):
                        kv_home(layer, which).start()

                @pl.when(layer == x)
                def _():
                    kv_keep(layer, x)

    def forward_far(u):
        @pl.when(x > 0)
        def _():
            wait_for(far_in.at[0, u], far_recv.at[0, u])

        carried = stack_heads(far_in[0, u]).astype(jnp.float32)
        forward_task(FAR, u, opposite, jnp.where(x == 0, 0.0, carried))
        keep(0, FAR, opposite, u)

    def backward_far(u):
        wait_for(far_in.at[1, u], far_recv.at[1, u])
        backward_task(FAR, u, far_in[1, u], True)
        keep(1, FAR, opposite, u)

    for u in range(NU):
        wait_for(gin.at[u], b_recv.at[u])

    forward_own(0)
    backward_own(0)
    home_move(0, 0).start()
    forward_own(1)
    pass_on(0, 0)
    backward_own(1)
    pass_on(0, 1)
    home_move(1, 0).start()
    pass_on(1, 0)
    home_move(1, 1).start()
    forward_far(0)
    home_move(0, 1).start()
    forward_far(1)
    backward_far(0)
    kv_own()
    backward_far(1)
    pass_on(1, 1)
    kv_sums(FAR)
    kv_keep(FAR, opposite)

    @pl.when(edge)
    def _():
        for g in others:
            for which in range(2):
                edge_move(g, which).wait_send()

    for other in others:
        for which in range(2):
            kv_move(other, which).wait_send()
        for u in range(NU):
            q_move(other, u).wait_send()
    for other in (after, before):
        for which in range(2):
            kv_home(other, which).wait_send()
    for u in range(NU):
        for kind in range(2):
            home_move(kind, u).wait_send()
            near_move(kind, u).wait_send()

            if kind == 0 or u < DIRECT:

                @pl.when(more[kind])
                def _():
                    far_move(kind, u).wait_send()

        if u >= DIRECT:

            @pl.when(opposite < LAYERS - 1)
            def _():
                direct_move(u).wait_send()

    for slot in range(SLOTS):

        @pl.when(jnp.logical_and(jnp.logical_not(last_shard), hands_on(slot)))
        def _():
            for which in range(2):
                halo(slot, which).wait_send()

        @pl.when(jnp.logical_and(slot != opposite, jnp.logical_not(first_shard)))
        def _():
            part_copy(slot).wait_send()

    kept = pl.ds(0, TOK * (LAYERS - 1) // LAYERS)
    for kind, dst in enumerate((att_hbm, qg_hbm)):
        wait_for(dst.at[:, kept], home_recv.at[kind])
    for which, dst in enumerate((kg_hbm, vg_hbm)):
        wait_for(dst, home_recv.at[2 + which])


def settle(*refs):
    copies = [pltpu.make_async_copy(refs[i], refs[4 + i], refs[8].at[i]) for i in range(4)]
    for copy in copies:
        copy.start()
    for copy in copies:
        copy.wait()


def shards(query_in, key_in, value_in, doc_ids, out_grad):
    shards_n = lax.axis_size("ctx")
    bf16, f32 = jnp.bfloat16, jnp.float32
    feat, kv = HEADS * HD, KVH * HD
    hbm = pl.BlockSpec(memory_space=pl.ANY)
    dma = pltpu.SemaphoreType.DMA
    att, qg, kg, vg = pl.pallas_call(
        functools.partial(kernel, shards_n),
        out_shape=(
            pltpu.VMEM((MB, TOK, feat), bf16),
            pltpu.VMEM((MB, TOK, feat), bf16),
            pltpu.VMEM((MB, TOK, kv), bf16),
            pltpu.VMEM((MB, TOK, kv), bf16),
        ),
        in_specs=[hbm] * 5,
        out_specs=[pl.BlockSpec(memory_space=pltpu.VMEM)] * 4,
        scratch_shapes=[
            pltpu.VMEM((SLOTS, NU, TOK, COLS), bf16),
            pltpu.VMEM((NU, TOK, COLS), bf16),
            pltpu.VMEM((2, NU, TOK, COLS), bf16),
            pltpu.VMEM((SLOTS, NU, TOK, COLS), bf16),
            pltpu.VMEM((SLOTS, NU, TOK, COLS), bf16),
            pltpu.VMEM((SLOTS, NU, ROWS, HD), bf16),
            pltpu.VMEM((SLOTS, NU, ROWS, TOK), f32),
            pltpu.VMEM((SLOTS, NU, ROWS, 2 * TOK), bf16),
            pltpu.VMEM((SLOTS, 2 * TOK, HD), bf16),
            pltpu.VMEM((SLOTS, 2 * TOK, HD), bf16),
            pltpu.VMEM((MB, TOK, TOK), f32),
            pltpu.VMEM((MB, TOK), jnp.int32),
            pltpu.VMEM((MB, TOK), jnp.int32),
            pltpu.VMEM((SLOTS, HD, 2 * TOK), f32),
            pltpu.VMEM((SLOTS, HD, 2 * TOK), f32),
            pltpu.VMEM((SLOTS, 2, HD, TOK), bf16),
            pltpu.VMEM((SLOTS, 2, HD, TOK), bf16),
            pltpu.VMEM((SLOTS, 2, TOK, HD), bf16),
            dma((2,)),
            dma((NGRP * NU,)),
            dma((SLOTS * NU,)),
            dma((2 * NGRP,)),
            dma((2 * SLOTS,)),
            dma((2 * SLOTS,)),
            dma((2 * SLOTS,)),
            dma((NU,)),
            dma((SLOTS,)),
            dma((SLOTS,)),
            dma((4, LAYERS * NU)),
            dma((4,)),
            dma((2, NU)),
            dma((2, NU)),
            dma((2, NU)),
            dma((2, NU)),
            dma((NU,)),
        ],
        compiler_params=pltpu.CompilerParams(
            collective_id=0, has_side_effects=True, vmem_limit_bytes=32 * 1024 * 1024
        ),
        cost_estimate=pl.CostEstimate(flops=2_000_000_000, bytes_accessed=5_000_000, transcendentals=600_000),
    )(*[pltpu.with_memory_space_constraint(a, pltpu.HBM) for a in (query_in[0], key_in[0], value_in[0], doc_ids, out_grad)])
    att, qg, kg, vg = pl.pallas_call(
        settle,
        out_shape=[jax.ShapeDtypeStruct(a.shape, a.dtype) for a in (att, qg, kg, vg)],
        in_specs=[hbm] * 4,
        out_specs=[hbm] * 4,
        scratch_shapes=[dma((4,))],
        compiler_params=pltpu.CompilerParams(vmem_limit_bytes=1 * 1024 * 1024),
    )(att, qg, kg, vg)
    return (att[None], qg[None], kg[None], vg[None])


def solution(mesh):
    split = P("section", None, "ctx", None)
    return jax.shard_map(
        shards,
        mesh=mesh,
        in_specs=(split, split, split, P(), P(None, "ctx", None)),
        out_specs=(split, split, split, split),
        check_vma=False,
    )
```
